256 devices in a mesh: ctx: 32 (over x_lo, z, core), head: 8 (over y, x_hi).
Axes of the slice: x: 4 (x_hi: 2, x_lo: 2; x = x_hi * 2 + x_lo), y: 4, z: 8, core: 2. Of those that a mesh axis runs over, the one named last changes fastest.
Arguments:
- queries: bfloat16 [4096, 16384], P('ctx', 'head'), may hold values from -8 to 8
- seg_keys: bfloat16 [4096, 1024], P('ctx', 'head'), may hold values from -6 to 6
- seg_values: bfloat16 [4096, 1024], P('ctx', 'head'), may hold values from -6 to 6
- cache_keys: bfloat16 [1024, 1024], P('ctx', 'head'), may hold values from -8 to 8
- cache_values: bfloat16 [1024, 1024], P('ctx', 'head'), may hold values from -6 to 6
- span_order: int32 [64], replicated, may hold values from 0 to 63, each once
- cache_length: int32 [1], replicated, may hold values from 128 to 1024
- out_weight: bfloat16 [16384, 16384], P('head', 'ctx'), may hold values from -1.5 to 1.5
Outputs:
- mixed: bfloat16 [4096, 16384], P('head', 'ctx')
- page_min: bfloat16 [256, 1024], P('ctx', 'head')
- page_max: bfloat16 [256, 1024], P('ctx', 'head')
The draws below stay inside these ranges and needn't reach their ends.
All inputs are finite; a program needn't handle non-finite values.
Results may differ from the reference program's by a relative error of at most 0.019.
Values may be sent and summed in bfloat16 or wider, within the bound.
No kernel may reach another device: no remote copies, remote signals or barrier semaphores. Data moves between devices by JAX's collectives and lax.ppermute only.
A program may use at most 128 MiB of HBM per device.

```python
import math
import jax
import jax.numpy as jnp
from jax import lax

D = 16384
HD = 128
GROUP = 16
PAGE = 16
KV_HEADS = 8
HEADS = 128
TOKENS = 4096
SPAN = 64
SPANS = 64
CACHE = 1024
PAGES = 256


def draw_queries(key, part):
    key = jax.random.fold_in(key, 11)
    sample_key = jax.random.fold_in(key, 0)
    sample = jax.random.normal(sample_key, (TOKENS, HEADS, HD), jnp.float32)
    return jnp.clip(sample, -8.0, 8.0).reshape(TOKENS, HEADS * HD).astype(jnp.bfloat16)


def draw_cache_keys(key, part):
    key = jax.random.fold_in(key, 12)
    sample_key = jax.random.fold_in(key, 0)
    sample = jax.random.normal(sample_key, (CACHE, KV_HEADS, HD), jnp.float32)
    return jnp.clip(sample, -8.0, 8.0).reshape(CACHE, KV_HEADS * HD).astype(jnp.bfloat16)


def block_levels(own_key, dims, pieces, low, top_value):
    def one(axis_at, blocks):
        heights = jax.random.uniform(jax.random.fold_in(jax.random.fold_in(own_key, 6), axis_at), (blocks,), jnp.float32, low / len(pieces), top_value / len(pieces))
        return jnp.repeat(jnp.exp(heights), dims[axis_at] // blocks).reshape((-1,) + (1,) * (len(dims) - axis_at - 1))

    factor_of = one(*pieces[0])
    for cut in pieces[1:]:
        factor_of = factor_of * one(*cut)
    return factor_of


def normal_values(stream_key, shape, deviation, bound, cuts=(), kind=jnp.bfloat16):
    factor_of = block_levels(stream_key, shape, cuts, -0.22, 0.18) if cuts else 1.0
    result = jax.random.normal(stream_key, shape, jnp.float32) * deviation * factor_of
    return jnp.minimum(jnp.maximum(result, -bound), bound).astype(kind)


def setup_inputs(seed: int = 0) -> dict:
    arg_keys = jax.random.split(jax.random.key(seed), 9)
    queries = draw_queries(jax.random.fold_in(arg_keys[8], 71), 0)
    seg_keys = normal_values(arg_keys[1], (TOKENS, KV_HEADS * HD), 1.0, 6.0, ((0, 32), (1, 8)))
    seg_values = normal_values(arg_keys[2], (TOKENS, KV_HEADS * HD), 1.0, 6.0, ((0, 32), (1, 8)))
    cache_keys = draw_cache_keys(jax.random.fold_in(arg_keys[8], 71), 0)
    cache_values = normal_values(arg_keys[4], (CACHE, KV_HEADS * HD), 1.0, 6.0, ((0, 32), (1, 8)))
    span_order = jax.random.permutation(arg_keys[5], SPANS).astype(jnp.int32)
    cache_length = jax.random.randint(arg_keys[6], (1,), CACHE // 8, CACHE + 1).astype(jnp.int32)
    out_weight = normal_values(arg_keys[7], (HEADS * HD, D), 0.25, 1.5, ((0, 8), (1, 32)))
    return {"queries": queries, "seg_keys": seg_keys, "seg_values": seg_values, "cache_keys": cache_keys, "cache_values": cache_values, "span_order": span_order, "cache_length": cache_length, "out_weight": out_weight}


def reference(queries, seg_keys, seg_values, cache_keys, cache_values, span_order, cache_length, out_weight):
    row_index = jnp.arange(TOKENS, dtype=jnp.int32)
    positions = span_order[row_index // SPAN] * SPAN + row_index % SPAN
    causal = positions[None, :] <= positions[:, None]
    valid = jnp.arange(CACHE, dtype=jnp.int32) < cache_length[0]
    score_scale = 1.0 / math.sqrt(HD)

    def one_head(head_index):
        kv_index = head_index // GROUP
        query_head = lax.dynamic_slice_in_dim(queries, head_index * HD, HD, 1)
        seg_key = lax.dynamic_slice_in_dim(seg_keys, kv_index * HD, HD, 1)
        seg_value = lax.dynamic_slice_in_dim(seg_values, kv_index * HD, HD, 1)
        cache_key = lax.dynamic_slice_in_dim(cache_keys, kv_index * HD, HD, 1)
        cache_value = lax.dynamic_slice_in_dim(cache_values, kv_index * HD, HD, 1)
        seg_scores = jnp.dot(query_head, seg_key.T, preferred_element_type=jnp.float32) * score_scale
        cache_scores = jnp.dot(query_head, cache_key.T, preferred_element_type=jnp.float32) * score_scale
        seg_scores = jnp.where(causal, seg_scores, -1e+30)
        cache_scores = jnp.where(valid[None, :], cache_scores, -1e+30)
        row_peak = jnp.maximum(lax.optimization_barrier(jnp.max(seg_scores, axis=1)), lax.optimization_barrier(jnp.max(cache_scores, axis=1)))
        seg_weights = jnp.where(causal, jnp.exp(seg_scores - row_peak[:, None]), 0.0)
        cache_weights = jnp.where(valid[None, :], jnp.exp(cache_scores - row_peak[:, None]), 0.0)
        denominator = lax.optimization_barrier(jnp.sum(seg_weights, axis=1)) + lax.optimization_barrier(jnp.sum(cache_weights, axis=1))
        combined = jnp.dot(seg_weights.astype(jnp.bfloat16), seg_value, preferred_element_type=jnp.float32)
        combined = combined + jnp.dot(cache_weights.astype(jnp.bfloat16), cache_value, preferred_element_type=jnp.float32)
        return (combined / denominator[:, None]).astype(jnp.bfloat16)
    per_head = lax.map(one_head, jnp.arange(HEADS, dtype=jnp.int32))
    attended = jnp.transpose(per_head, (1, 0, 2)).reshape(TOKENS, HEADS * HD)
    mixed = jnp.dot(attended, out_weight, preferred_element_type=jnp.float32).astype(jnp.bfloat16)
    paged_keys = seg_keys.reshape(PAGES, PAGE, KV_HEADS * HD)
    return (mixed, lax.optimization_barrier(jnp.min(paged_keys, axis=1)), lax.optimization_barrier(jnp.max(paged_keys, axis=1)))
```

```python
import functools
import math

import jax
import jax.numpy as jnp
from jax import lax
from jax.experimental import pallas as pl
from jax.experimental.pallas import tpu as pltpu
from jax.sharding import Mesh
from jax.sharding import PartitionSpec as P

HD = 128
GROUP = 16
PAGE = 16
SPAN = 64
NZ = 8
CHUNKS = 1
ROWS = SPAN // CHUNKS
WIDTH = GROUP * HD
TILE_HEADS = 512 // ROWS if 512 // ROWS < GROUP else GROUP
LOG2E = 1.4426950408889634
HIDDEN = -1e30
KEYS = 640
F32 = jnp.float32
BF16 = jnp.bfloat16


def shift(block, axis, distance):
    n = lax.axis_size(axis)
    return lax.ppermute(block, axis, [(i, (i + distance) % n) for i in range(n)])


def flip(block, axis):
    return shift(block, axis, 1)


def flip_both(block):
    return lax.ppermute(block, ("xlo", "core"), [(i, 3 - i) for i in range(4)])


def outward(block):
    route = []
    for z in range(NZ):
        route.append((2 * z, 2 * ((z + 1) % NZ)))
        route.append((2 * z + 1, 2 * ((z - 1) % NZ) + 1))
    return lax.ppermute(block, ("z", "core"), route)


def attention_kernel(
    meta, order, length, q_own, q_got, *rest, scale
):
    kv_refs, out_ref, k_scr, v_scr, s_scr, m_scr = rest[:9], rest[9], rest[10], rest[11], rest[12], rest[13]
    step = pl.program_id(0)
    xlo, z, core = meta[0], meta[1], meta[2]
    tile_rows = ROWS * TILE_HEADS
    tiles_per_span = GROUP // TILE_HEADS
    tiles = 2 * tiles_per_span

    own, ring, ring4, crossed, crossed4 = kv_refs[0], kv_refs[1:4], kv_refs[4], kv_refs[5:8], kv_refs[8]

    def place(slot, part, source, index):
        k_scr[slot, :, part * HD : (part + 1) * HD] = source[index, 0:128, :].T
        v_scr[slot, part * 128 : part * 128 + 128, 0:HD] = source[index, 128:256, :]
        v_scr[slot, 512 + part * 32 : 544 + part * 32, 0:HD] = source[index, 288:320, :]

    def place_cache(slot, sources):
        keys = jnp.concatenate([source[index, 256:288, :] for source, index in sources], axis=0)
        k_scr[slot, :, 512:640] = keys.T

    @pl.when(step == 0)
    def _():
        lists = [[(own, i) for i in range(4)]]
        lists += [[(r, i) for i in range(4)] for r in ring]
        lists += [[(ring4, 0), (ring4, 1), (crossed4, 0), (crossed4, 1)]]
        lists += [[(r, i) for i in range(4)] for r in crossed]
        for slot, sources in enumerate(lists):
            for part, (source, index) in enumerate(sources):
                place(slot, part, source, index)
            place_cache(slot, sources)
        lane = lax.broadcasted_iota(jnp.int32, (NZ, KEYS, HD), 2)
        v_scr[:, :, HD:] = jnp.where(lane == 0, 1.0, 0.0).astype(BF16)

    def source_of(slot, part):
        is_crossed = jnp.int32(slot > 4)
        distance = jnp.where(slot > 4, slot - 4, slot)
        sign = jnp.where(core == 0, -1, 1) * jnp.where(slot > 4, -1, 1)
        sz = (z + sign * distance + NZ) % NZ
        half_b, half_a = part // 2, part % 2
        sx = (xlo + half_a) % 2
        sc = (core + half_b + is_crossed) % 2
        return sx * 16 + sz * 2 + sc

    lane128 = lax.broadcasted_iota(jnp.int32, (1, 128), 1)

    def key_places(slot):
        pieces = []
        cache_slot = lane128 % 32
        for part in range(4):
            ctx = source_of(slot, part)
            pieces.append(jnp.where(lane128 < SPAN, order[2 * ctx], order[2 * ctx + 1]))
            cache_slot = jnp.where(lane128 // 32 == part, cache_slot + ctx * 32, cache_slot)
        pieces.append(jnp.where(cache_slot < length[0], -1, 64))
        return jnp.concatenate(pieces, axis=1)

    def first_pass():
        span = step // tiles_per_span
        group = step % tiles_per_span
        own_place = order[2 * (xlo * 16 + z * 2 + core) + xlo]
        got_place = order[2 * ((1 - xlo) * 16 + z * 2 + core) + xlo]
        mine = span == xlo
        my_place = jnp.where(mine, own_place, got_place)
        q_rows = jnp.where(mine, q_own[...], q_got[...])
        q_tile = jnp.concatenate([q_rows[:, i * HD : (i + 1) * HD] for i in range(TILE_HEADS)], axis=0)
        buffer = step % 2

        def scores_of(slot):
            return jnp.dot(q_tile, k_scr[slot], preferred_element_type=F32) * scale

        s = scores_of(0)
        places = key_places(0)
        lane = lax.broadcasted_iota(jnp.int32, (1, KEYS), 1) % SPAN
        row = lax.broadcasted_iota(jnp.int32, (tile_rows, 1), 0) % ROWS + meta[3]
        bias = jnp.where(places < my_place, 0.0, HIDDEN)
        diag = jnp.where(places == my_place, lane, 1000)
        s = jnp.where(diag <= row, s, s + bias)
        s_scr[buffer, 0] = s
        return buffer, my_place, scores_of, s

    def body(do_first, do_second):
        if do_first:
            buffer, my_place, scores_of, s0 = first_pass()
            peak = functools.reduce(jnp.maximum, [s0[:, i * 128 : (i + 1) * 128] for i in range(5)])
        if do_second:
            old = (step + 1) % 2
            top = m_scr[old]
            acc = jnp.zeros((tile_rows, 2 * HD), F32)
        for slot in range(NZ):
            if do_first and slot > 0:
                s = scores_of(slot) + jnp.where(key_places(slot) < my_place, 0.0, HIDDEN)
                s_scr[buffer, slot] = s
                peak = functools.reduce(jnp.maximum, [s[:, i * 128 : (i + 1) * 128] for i in range(5)], peak)
            if do_second:
                weights = jnp.concatenate(
                    [jnp.exp2(s_scr[old, slot, :, i * 128 : (i + 1) * 128] - top) for i in range(5)], axis=1
                ).astype(BF16)
                acc = acc + jnp.dot(weights, v_scr[slot], preferred_element_type=F32)
        if do_first:
            m_scr[buffer] = jnp.broadcast_to(jnp.max(peak, axis=1, keepdims=True), (tile_rows, 128))
        if do_second:
            result = (acc[:, :HD] / acc[:, HD : HD + 1]).astype(BF16)
            for i in range(TILE_HEADS):
                out_ref[0, :, i * HD : (i + 1) * HD] = result[i * ROWS : (i + 1) * ROWS]

    pl.when(step == 0)(lambda: body(True, False))
    pl.when((step > 0) & (step < tiles))(lambda: body(True, True))
    pl.when(step == tiles)(lambda: body(False, True))


def attention(meta, order, length, q_own, q_got, kv_blocks):
    tiles_per_span = GROUP // TILE_HEADS
    tiles = 2 * tiles_per_span
    width = TILE_HEADS * HD
    tile_rows = ROWS * TILE_HEADS

    def q_map(step, *_):
        return (0, jnp.minimum(step, tiles - 1) % tiles_per_span)

    def out_map(step, *_):
        tile = jnp.maximum(step - 1, 0)
        return (tile // tiles_per_span, 0, tile % tiles_per_span)

    whole = [pl.BlockSpec(b.shape, lambda step, *_: (0, 0, 0)) for b in kv_blocks]
    return pl.pallas_call(
        functools.partial(attention_kernel, scale=LOG2E / math.sqrt(HD)),
        out_shape=jax.ShapeDtypeStruct((2, ROWS, WIDTH), BF16),
        grid_spec=pltpu.PrefetchScalarGridSpec(
            num_scalar_prefetch=3,
            grid=(tiles + 1,),
            in_specs=[pl.BlockSpec((ROWS, width), q_map), pl.BlockSpec((ROWS, width), q_map)] + whole,
            out_specs=pl.BlockSpec((1, ROWS, width), out_map),
            scratch_shapes=[
                pltpu.VMEM((NZ, HD, KEYS), BF16),
                pltpu.VMEM((NZ, KEYS, 2 * HD), BF16),
                pltpu.VMEM((2, NZ, tile_rows, KEYS), F32),
                pltpu.VMEM((2, tile_rows, 128), F32),
            ],
        ),
        compiler_params=pltpu.CompilerParams(vmem_limit_bytes=48 * 1024 * 1024),
        cost_estimate=pl.CostEstimate(flops=2 * 2 * 2 * ROWS * GROUP * 5120 * 256, bytes_accessed=4 * 2**20, transcendentals=2 * ROWS * GROUP * 5120),
        name="attention",
    )(meta, order, length, q_own, q_got, *kv_blocks)


def project_kernel(meta, *refs):
    a_refs, w_refs, outs = refs[:9], refs[9:13], refs[13:20]
    a_scr, sem = refs[20], refs[21]
    z, y = meta[1], meta[2]
    step = pl.program_id(0)

    @pl.when(step == 0)
    def _():
        copies = []

        def bring(source, s, distance):
            place = (z + distance + NZ) % NZ
            part = (2 * s + place // 4 - y + 4) % 4
            copies.append(pltpu.make_async_copy(source, a_scr.at[part, place % 4], sem.at[len(copies)]))

        for s in range(2):
            bring(a_refs[0].at[s], s, 0)
            for d in range(1, 4):
                bring(a_refs[d].at[s], s, -d)
                bring(a_refs[3 + d].at[s], s, d)
        bring(a_refs[7].at[0], 0, 4)
        bring(a_refs[8].at[0], 1, 4)
        for c in copies:
            c.start()
        for c in copies:
            c.wait()

    rows = a_scr[...].reshape(16 * ROWS, WIDTH)
    xhi = meta[3]
    for i, w in enumerate(w_refs):

        @pl.when(step == i)
        def _():
            part = jnp.dot(rows, w[...], preferred_element_type=F32).reshape(4, 2, 2, ROWS, 512)
            part = part.reshape(4, 2, 2 * ROWS, 512)

            def store(out, y_part, first, second):
                value = part[y_part]
                a = jnp.where(xhi == 0, value[0], value[1])
                b = jnp.where(xhi == 0, value[1], value[0])
                if first is not None:
                    outs[first][...] = a.astype(BF16)
                if second is not None:
                    outs[second][...] = b.astype(BF16)

            own = part[0]
            a = jnp.where(xhi == 0, own[0], own[1])
            b = jnp.where(xhi == 0, own[1], own[0])
            outs[0][...] = jnp.concatenate([a, b], axis=0).astype(BF16)
            store(outs, 1, 1, 2)
            store(outs, 2, 3, 4)
            store(outs, 3, 5, 6)


def project(meta, blocks, weights):
    whole = pl.BlockSpec(memory_space=pl.ANY)
    resident = pl.BlockSpec((WIDTH, 512), lambda step, *_: (0, 0))
    shapes = [(4 * ROWS, 2048)] + [(2 * ROWS, 2048)] * 6
    return pl.pallas_call(
        project_kernel,
        out_shape=[jax.ShapeDtypeStruct(s, BF16) for s in shapes],
        grid_spec=pltpu.PrefetchScalarGridSpec(
            num_scalar_prefetch=1,
            grid=(4,),
            in_specs=[whole] * 9 + [resident] * 4,
            out_specs=[pl.BlockSpec((s[0], 512), lambda step, *_: (0, step)) for s in shapes],
            scratch_shapes=[
                pltpu.VMEM((4, 4, ROWS, WIDTH), BF16),
                pltpu.SemaphoreType.DMA((16,)),
            ],
        ),
        compiler_params=pltpu.CompilerParams(vmem_limit_bytes=48 * 1024 * 1024),
        cost_estimate=pl.CostEstimate(flops=2 * 16 * ROWS * 2048 * 2048, bytes_accessed=16 * 2**20, transcendentals=0),
        name="project",
    )(meta, *blocks, *weights)


def add2(x, y):
    return (x.astype(F32) + y.astype(F32)).astype(BF16)


def last_sum_kernel(x, y, z, u, *outs):
    total = x[...].astype(F32) + y[...].astype(F32) + z[...].astype(F32) + u[...].astype(F32)
    for i, out in enumerate(outs):
        out[...] = total[:, 512 * i : 512 * (i + 1)].astype(BF16)


def last_sum(*terms):
    rows = 2 * ROWS
    return pl.pallas_call(
        last_sum_kernel,
        out_shape=[jax.ShapeDtypeStruct((rows, 512), BF16)] * 4,
        in_specs=[pl.BlockSpec((rows, 2048), lambda: (0, 0))] * 4,
        out_specs=[pl.BlockSpec((rows, 512), lambda: (0, 0))] * 4,
        compiler_params=pltpu.CompilerParams(vmem_limit_bytes=32 * 1024 * 1024),
        name="last_sum",
    )(*terms)


def assemble_kernel(meta, *refs):
    pieces, out, sem = refs[:-2], refs[-2], refs[-1]
    xlo, core = meta[0], meta[1]
    copies = []
    for j in range(CHUNKS):
        for i in range(4):
            from_core = (core + i % 2) % 2
            from_xlo = (xlo + i // 2) % 2
            for zi in range(2):
                row = (zi * 2 + from_core) * 128 + from_xlo * SPAN + j * ROWS
                copies.append(
                    pltpu.make_async_copy(
                        pieces[4 * j + i].at[pl.ds(zi * ROWS, ROWS)],
                        out.at[pl.ds(pl.multiple_of(row, 32), ROWS)],
                        sem.at[len(copies)],
                    )
                )
    for c in copies:
        c.start()
    for c in copies:
        c.wait()


def assemble(meta, pieces):
    return pl.pallas_call(
        assemble_kernel,
        out_shape=jax.ShapeDtypeStruct((512, 512), BF16),
        grid_spec=pltpu.PrefetchScalarGridSpec(
            num_scalar_prefetch=1,
            grid=(1,),
            in_specs=[pl.BlockSpec(memory_space=pl.ANY)] * (4 * CHUNKS),
            out_specs=pl.BlockSpec(memory_space=pl.ANY),
            scratch_shapes=[pltpu.SemaphoreType.DMA((8 * CHUNKS,))],
        ),
        name="assemble",
    )(meta, *pieces)


def shards(
    queries, seg_keys, seg_values, cache_keys, cache_values, span_order, cache_length, out_weight
):
    xlo, z, core = lax.axis_index("xlo"), lax.axis_index("z"), lax.axis_index("core")
    y, xhi = lax.axis_index("y"), lax.axis_index("xhi")

    packed = jnp.concatenate([seg_keys, seg_values, cache_keys, cache_values], axis=0)
    kv_core, kv_xlo, kv_both = flip(packed, "core"), flip(packed, "xlo"), flip_both(packed)
    kv_own = jnp.stack([packed, kv_xlo, kv_core, kv_both])
    ring, crossed = [], []
    block = kv_own
    for _ in range(3):
        block = outward(block)
        ring.append(block)
        crossed.append(flip(block, "core"))
    ring4 = outward(block[:2])
    crossed4 = flip(ring4, "core")
    kv_blocks = [kv_own, *ring, ring4, *crossed, crossed4]

    give = lax.dynamic_slice_in_dim(queries, (1 - xlo) * SPAN, SPAN, 0)
    q_got = flip(give, "xlo")
    q_own = lax.dynamic_slice_in_dim(queries, xlo * SPAN, SPAN, 0)

    w_core = flip(out_weight, "core")
    w_xlo = flip(out_weight, "xlo")
    w_both = flip(w_xlo, "core")
    weights = [out_weight, w_core, w_xlo, w_both]

    pieces = []
    for j in range(CHUNKS):
        attended = attention(
            jnp.stack([xlo, z, core, jnp.int32(j * ROWS)]),
            span_order,
            cache_length,
            q_own[j * ROWS : (j + 1) * ROWS],
            q_got[j * ROWS : (j + 1) * ROWS],
            kv_blocks,
        )
        ahead, behind = [], []
        up = down = attended
        for _ in range(3):
            up, down = shift(up, "z", 1), shift(down, "z", -1)
            behind.append(up)
            ahead.append(down)
        far = [shift(up[:1], "z", 1), shift(down[1:], "z", -1)]
        own, p1a, p1b, p2a, p2b, p3a, p3b = project(
            jnp.stack([xlo, z, y, xhi]), [attended, *behind, *ahead, *far], weights
        )
        far_a, far_b = shift(p2a, "y", 1), shift(p2b, "y", -1)
        in1b, in3a = shift(p1b, "y", 1), shift(p3a, "y", -1)
        in1a, in3b = shift(add2(p1a, far_a), "y", 1), shift(add2(p3b, far_b), "y", -1)
        own_a, own_b = own[: 2 * ROWS], own[2 * ROWS :]
        give_b = (own_b.astype(F32) + in1b.astype(F32) + in3b.astype(F32)).astype(BF16)
        got_a = flip(give_b, "xhi")
        mine, to_core, to_xlo, to_both = last_sum(own_a, in1a, in3a, got_a)
        pieces += [mine, flip(to_core, "core"), flip(to_xlo, "xlo"), flip_both(to_both)]
    mixed = assemble(jnp.stack([xlo, core]), pieces)
    paged_keys = seg_keys.reshape(seg_keys.shape[0] // PAGE, PAGE, seg_keys.shape[1])
    return (mixed, jnp.min(paged_keys, axis=1), jnp.max(paged_keys, axis=1))


def solution(mesh):
    split = Mesh(mesh.devices.reshape(2, NZ, 2, 4, 2), ("xlo", "z", "core", "y", "xhi"))
    ctx, head = ("xlo", "z", "core"), ("y", "xhi")
    in_specs = (
        P(ctx, head),
        P(ctx, head),
        P(ctx, head),
        P(ctx, head),
        P(ctx, head),
        P(),
        P(),
        P(head, ctx),
    )
    out_specs = (P(head, ctx), P(ctx, head), P(ctx, head))
    return jax.shard_map(shards, mesh=split, in_specs=in_specs, out_specs=out_specs, check_vma=False)
```

```python
import functools
import math

import jax
import jax.numpy as jnp
from jax import lax
from jax.experimental import pallas as pl
from jax.experimental.pallas import tpu as pltpu
from jax.sharding import Mesh
from jax.sharding import PartitionSpec as P

HD = 128
GROUP = 16
PAGE = 16
SPAN = 64
NZ = 8
CHUNKS = 2
ROWS = SPAN // CHUNKS
WIDTH = GROUP * HD
LOG2E = 1.4426950408889634
HIDDEN = -1e30
KEYS = 640
F32 = jnp.float32
BF16 = jnp.bfloat16


def shift(block, axis, distance):
    n = lax.axis_size(axis)
    return lax.ppermute(block, axis, [(i, (i + distance) % n) for i in range(n)])


def flip(block, axis):
    return shift(block, axis, 1)


def flip_both(block):
    return lax.ppermute(block, ("xlo", "core"), [(i, 3 - i) for i in range(4)])


def outward(block):
    route = []
    for z in range(NZ):
        route.append((2 * z, 2 * ((z + 1) % NZ)))
        route.append((2 * z + 1, 2 * ((z - 1) % NZ) + 1))
    return lax.ppermute(block, ("z", "core"), route)


def pack_kernel(k, v, ck, cv, out):
    out[0:128] = k[...].T
    out[128:256] = v[...]
    out[256:288] = ck[...]
    out[288:320] = cv[...]


def pack(k, v, ck, cv):
    return pl.pallas_call(
        pack_kernel,
        out_shape=jax.ShapeDtypeStruct((320, HD), BF16),
        name="pack",
    )(k, v, ck, cv)


def attention_kernel(meta, order, length, q_own, q_got, *rest, slots, scale, first, last, chunk):
    n_refs = 1 + max(part[0] for slot in slots for part in slot)
    kv_refs, rest = rest[:n_refs], rest[n_refs:]
    if not first:
        top_in, acc_in, rest = rest[0], rest[1], rest[2:]
    tile = pl.program_id(0)
    span = tile % 2
    xlo, z, core = meta[0], meta[1], meta[2]
    first_row = (chunk if last else tile // 2) * ROWS
    lane128 = lax.broadcasted_iota(jnp.int32, (1, 128), 1)

    def source_of(side, part, distance):
        sign = jnp.where((core + side) % 2 == 0, -1, 1)
        sz = (z + sign * distance + NZ) % NZ
        return ((xlo + part % 2) % 2) * 16 + sz * 2 + (core + part // 2 + side) % 2

    own_place = order[2 * (xlo * 16 + z * 2 + core) + xlo]
    got_place = order[2 * ((1 - xlo) * 16 + z * 2 + core) + xlo]
    mine = span == xlo
    my_place = jnp.where(mine, own_place, got_place)
    q_rows = jnp.where(mine, q_own[...], q_got[...])
    halves = 2
    half_heads = GROUP // halves
    half_rows = half_heads * ROWS
    q_tiles = [
        jnp.concatenate([q_rows[:, i * HD : (i + 1) * HD] for i in range(h * half_heads, (h + 1) * half_heads)], axis=0)
        for h in range(halves)
    ]
    tops = [None if first else top_in[h * half_rows : (h + 1) * half_rows] for h in range(halves)]
    accs = [None if first else acc_in[h * half_rows : (h + 1) * half_rows] for h in range(halves)]

    for slot in slots:
        parts = [kv_refs[ref].at[place] for ref, place, *_ in slot]
        keys = jnp.concatenate(
            [p[0:128] for p in parts] + [jnp.concatenate([p[256:288] for p in parts], axis=0).T], axis=1
        )
        values = jnp.concatenate([p[128:256] for p in parts] + [p[288:320] for p in parts], axis=0)
        values = jnp.concatenate([values, jnp.ones((KEYS, HD), BF16)], axis=1)
        places = []
        cache_slot = lane128 % 32
        for i, (_, _, side, part, distance) in enumerate(slot):
            ctx = source_of(side, part, distance)
            places.append(jnp.where(lane128 < SPAN, order[2 * ctx], order[2 * ctx + 1]))
            cache_slot = jnp.where(lane128 // 32 == i, cache_slot + ctx * 32, cache_slot)
        places.append(jnp.where(cache_slot < length[0], -1, 64))
        places = jnp.concatenate(places, axis=1)
        bias = jnp.where(places < my_place, 0.0, HIDDEN)
        has_diagonal = slot[0][4] == 0
        if has_diagonal:
            lane = lax.broadcasted_iota(jnp.int32, (1, KEYS), 1) % SPAN
            diagonal = jnp.where(places == my_place, lane, 1000)
            row = lax.broadcasted_iota(jnp.int32, (half_rows, 1), 0) % ROWS + first_row
        for h in range(halves):
            s = jnp.dot(q_tiles[h], keys, preferred_element_type=F32) * scale
            if has_diagonal:
                s = jnp.where(diagonal <= row, s, s + bias)
            else:
                s = s + bias
            peak = functools.reduce(jnp.maximum, [s[:, i * 128 : (i + 1) * 128] for i in range(5)])
            peak = jnp.broadcast_to(jnp.max(peak, axis=1, keepdims=True), (half_rows, 128))
            top = peak if tops[h] is None else jnp.maximum(tops[h], peak)
            weights = jnp.concatenate(
                [jnp.exp2(s[:, i * 128 : (i + 1) * 128] - top) for i in range(5)], axis=1
            ).astype(BF16)
            added = jnp.dot(weights, values, preferred_element_type=F32)
            if accs[h] is None:
                accs[h] = added
            else:
                factor = jnp.exp2(tops[h] - top)
                accs[h] = accs[h] * jnp.concatenate([factor, factor], axis=1) + added
            tops[h] = top

    if last:
        (out,) = rest
        for h in range(halves):
            result = (accs[h][:, :HD] / accs[h][:, HD:]).astype(BF16)
            for i in range(half_heads):
                col = (h * half_heads + i) * HD
                out[0, :, col : col + HD] = result[i * ROWS : (i + 1) * ROWS]
    else:
        top_out, acc_out = rest
        for h in range(halves):
            top_out[h * half_rows : (h + 1) * half_rows] = tops[h]
            acc_out[h * half_rows : (h + 1) * half_rows] = accs[h]


def attention(meta, order, length, q_own, q_got, kv_blocks, slots, state, chunk=None):
    last, first = chunk is not None, state is None
    tile_rows = ROWS * GROUP
    base = 2 * chunk if last else 0
    q_spec = pl.BlockSpec((ROWS, WIDTH), lambda step, *_: ((base + step) // 2, 0))
    whole = [pl.BlockSpec(b.shape, lambda step, *_: (0, 0, 0)) for b in kv_blocks]
    state_shapes = [jax.ShapeDtypeStruct((2 * CHUNKS * tile_rows, w), F32) for w in (HD, 2 * HD)]
    in_state = [pl.BlockSpec((tile_rows, w), lambda step, *_: (base + step, 0)) for w in (HD, 2 * HD)]
    if last:
        out_shape = jax.ShapeDtypeStruct((2, ROWS, WIDTH), BF16)
        out_specs = pl.BlockSpec((1, ROWS, WIDTH), lambda step, *_: (step, 0, 0))
    else:
        out_shape, out_specs = state_shapes, [pl.BlockSpec((tile_rows, w), lambda step, *_: (step, 0)) for w in (HD, 2 * HD)]
    tiles = 2 if last else 2 * CHUNKS
    work = tiles * tile_rows * KEYS * len(slots)
    return pl.pallas_call(
        functools.partial(attention_kernel, slots=slots, scale=LOG2E / math.sqrt(HD), first=first, last=last, chunk=chunk),
        out_shape=out_shape,
        grid_spec=pltpu.PrefetchScalarGridSpec(
            num_scalar_prefetch=3,
            grid=(tiles,),
            in_specs=[q_spec, q_spec] + whole + ([] if first else in_state),
            out_specs=out_specs,
        ),
        compiler_params=pltpu.CompilerParams(vmem_limit_bytes=40 * 1024 * 1024),
        cost_estimate=pl.CostEstimate(flops=work * 4 * 256, bytes_accessed=4 * 2**20, transcendentals=work),
        name="attention",
    )(meta, order, length, q_own, q_got, *kv_blocks, *([] if first else state))


def parts_of(ref, side, distance, count=4, offset=0):
    return [(ref, i, side, offset + i, distance) for i in range(count)]


def project_kernel(meta, *refs):
    a_refs, w_refs, outs = refs[:9], refs[9:13], refs[13:20]
    a_scr, w_scr, a_sem, w_sem = refs[20:]
    z, y, xhi = meta[1], meta[2], meta[3]
    step = pl.program_id(0)

    def w_copy(i):
        return pltpu.make_async_copy(w_refs[i], w_scr.at[i], w_sem.at[i])

    @pl.when(step == 0)
    def _():
        copies = []

        def bring(source, s, distance):
            place = (z + distance + NZ) % NZ
            part = (2 * s + place // 4 - y + 4) % 4
            inner = 2 * ((place // 2 + xhi) % 2) + place % 2
            copies.append(pltpu.make_async_copy(source, a_scr.at[part, inner], a_sem.at[len(copies)]))

        for s in range(2):
            bring(a_refs[0].at[s], s, 0)
            for d in range(1, 4):
                bring(a_refs[d].at[s], s, -d)
                bring(a_refs[3 + d].at[s], s, d)
        bring(a_refs[7].at[0], 0, 4)
        bring(a_refs[8].at[0], 1, 4)
        for c in copies:
            c.start()
        for i in range(4):
            w_copy(i).start()
        for c in copies:
            c.wait()

    for i in range(4):

        @pl.when(step == i)
        def _():
            w_copy(i).wait()

    rows = a_scr[...].reshape(16 * ROWS, WIDTH)
    total = jnp.dot(rows, w_scr[step], preferred_element_type=F32).astype(BF16)
    outs[0][...] = total[: 4 * ROWS]
    for k in range(6):
        outs[1 + k][...] = total[(4 + 2 * k) * ROWS : (6 + 2 * k) * ROWS]


def project(meta, blocks, weights):
    whole = pl.BlockSpec(memory_space=pl.ANY)
    shapes = [(4 * ROWS, 2048)] + [(2 * ROWS, 2048)] * 6
    return pl.pallas_call(
        project_kernel,
        out_shape=[jax.ShapeDtypeStruct(s, BF16) for s in shapes],
        grid_spec=pltpu.PrefetchScalarGridSpec(
            num_scalar_prefetch=1,
            grid=(4,),
            in_specs=[whole] * 13,
            out_specs=[pl.BlockSpec((s[0], 512), lambda step, *_: (0, step)) for s in shapes],
            scratch_shapes=[
                pltpu.VMEM((4, 4, ROWS, WIDTH), BF16),
                pltpu.VMEM((4, WIDTH, 512), BF16),
                pltpu.SemaphoreType.DMA((16,)),
                pltpu.SemaphoreType.DMA((4,)),
            ],
        ),
        compiler_params=pltpu.CompilerParams(vmem_limit_bytes=40 * 1024 * 1024),
        cost_estimate=pl.CostEstimate(flops=2 * 16 * ROWS * 2048 * 2048, bytes_accessed=16 * 2**20, transcendentals=0),
        name="project",
    )(meta, *blocks, *weights)


def add2(x, y):
    return (x.astype(F32) + y.astype(F32)).astype(BF16)


def last_sum_kernel(x, y, z, u, *outs):
    total = x[...].astype(F32) + y[...].astype(F32) + z[...].astype(F32) + u[...].astype(F32)
    for i, out in enumerate(outs):
        out[...] = total[:, 512 * i : 512 * (i + 1)].astype(BF16)


def last_sum(*terms):
    rows = 2 * ROWS
    return pl.pallas_call(
        last_sum_kernel,
        out_shape=[jax.ShapeDtypeStruct((rows, 512), BF16)] * 4,
        in_specs=[pl.BlockSpec((rows, 2048), lambda: (0, 0))] * 4,
        out_specs=[pl.BlockSpec((rows, 512), lambda: (0, 0))] * 4,
        compiler_params=pltpu.CompilerParams(vmem_limit_bytes=32 * 1024 * 1024),
        name="last_sum",
    )(*terms)


def assemble_kernel(meta, *refs):
    pieces, out = refs[:-1], refs[-1]
    xlo, core = meta[0], meta[1]
    for j in range(CHUNKS):
        for i in range(4):
            from_core = (core + i % 2) % 2
            from_xlo = (xlo + i // 2) % 2
            for zi in range(2):
                row = (zi * 2 + from_core) * 128 + from_xlo * SPAN + j * ROWS
                out[pl.ds(pl.multiple_of(row, 32), ROWS)] = pieces[4 * j + i][zi * ROWS : (zi + 1) * ROWS]


def assemble(meta, pieces):
    return pl.pallas_call(
        assemble_kernel,
        out_shape=jax.ShapeDtypeStruct((512, 512), BF16),
        grid_spec=pltpu.PrefetchScalarGridSpec(
            num_scalar_prefetch=1,
            grid=(1,),
            in_specs=[pl.BlockSpec((2 * ROWS, 512), lambda step, *_: (0, 0))] * (4 * CHUNKS),
            out_specs=pl.BlockSpec((512, 512), lambda step, *_: (0, 0)),
        ),
        name="assemble",
    )(meta, *pieces)


def shards(
    queries, seg_keys, seg_values, cache_keys, cache_values, span_order, cache_length, out_weight
):
    xlo, z, core = lax.axis_index("xlo"), lax.axis_index("z"), lax.axis_index("core")
    y, xhi = lax.axis_index("y"), lax.axis_index("xhi")

    packed = pack(seg_keys, seg_values, cache_keys, cache_values)
    kv_core, kv_xlo, kv_both = flip(packed, "core"), flip(packed, "xlo"), flip_both(packed)
    give = lax.dynamic_slice_in_dim(queries, (1 - xlo) * SPAN, SPAN, 0)
    q_own = lax.dynamic_slice_in_dim(queries, xlo * SPAN, SPAN, 0)
    give, kv_core, kv_xlo, kv_both = lax.optimization_barrier((give, kv_core, kv_xlo, kv_both))
    q_got = flip(give, "xlo")
    kv_own = jnp.stack([packed, kv_xlo, kv_core, kv_both])
    ring1 = outward(kv_own)
    cross1 = flip(ring1, "core")
    ring2 = outward(ring1)
    cross2 = flip(ring2, "core")
    ring3 = outward(ring2)
    cross3 = flip(ring3, "core")
    ring4 = outward(ring3[:2])
    cross4 = flip(ring4, "core")

    q_got, out_weight = lax.optimization_barrier((q_got, out_weight))
    w_core = flip(out_weight, "core")
    w_xlo = flip(out_weight, "xlo")
    w_both = flip(w_xlo, "core")
    weights = [out_weight, w_core, w_xlo, w_both]

    meta = jnp.stack([xlo, z, core])
    attend = functools.partial(attention, meta, span_order, cache_length, q_own, q_got)
    state = attend([kv_own, ring1], [parts_of(0, 0, 0), parts_of(1, 0, 1)], None)
    state = attend([ring2, cross1], [parts_of(0, 0, 2), parts_of(1, 1, 1)], state)
    state = attend([ring3, cross2], [parts_of(0, 0, 3), parts_of(1, 1, 2)], state)
    far_slots = [parts_of(0, 1, 3), parts_of(1, 0, 4, 2) + parts_of(2, 1, 4, 2)]
    meta_project = jnp.stack([xlo, z, y, xhi])

    pieces = []
    for j in range(CHUNKS):
        attended = attend([cross3, ring4, cross4], far_slots, state, j)
        ahead, behind = [], []
        up = down = attended
        for _ in range(3):
            up, down = shift(up, "z", 1), shift(down, "z", -1)
            behind.append(up)
            ahead.append(down)
        far = [shift(up[:1], "z", 1), shift(down[1:], "z", -1)]
        own, p1a, p1b, p2a, p2b, p3a, p3b = project(meta_project, [attended, *behind, *ahead, *far], weights)
        far_a, far_b = shift(p2a, "y", 1), shift(p2b, "y", -1)
        in1b, in3a = shift(p1b, "y", 1), shift(p3a, "y", -1)
        in1a, in3b = shift(add2(p1a, far_a), "y", 1), shift(add2(p3b, far_b), "y", -1)
        own_a, own_b = own[: 2 * ROWS], own[2 * ROWS :]
        give_b = (own_b.astype(F32) + in1b.astype(F32) + in3b.astype(F32)).astype(BF16)
        got_a = flip(give_b, "xhi")
        mine, to_core, to_xlo, to_both = last_sum(own_a, in1a, in3a, got_a)
        pieces += [mine, flip(to_core, "core"), flip(to_xlo, "xlo"), flip_both(to_both)]
    mixed = assemble(jnp.stack([xlo, core]), pieces)
    paged_keys = seg_keys.reshape(seg_keys.shape[0] // PAGE, PAGE, seg_keys.shape[1])
    return (mixed, jnp.min(paged_keys, axis=1), jnp.max(paged_keys, axis=1))


def solution(mesh):
    split = Mesh(mesh.devices.reshape(2, NZ, 2, 4, 2), ("xlo", "z", "core", "y", "xhi"))
    ctx, head = ("xlo", "z", "core"), ("y", "xhi")
    in_specs = (
        P(ctx, head),
        P(ctx, head),
        P(ctx, head),
        P(ctx, head),
        P(ctx, head),
        P(),
        P(),
        P(head, ctx),
    )
    out_specs = (P(head, ctx), P(ctx, head), P(ctx, head))
    return jax.shard_map(shards, mesh=split, in_specs=in_specs, out_specs=out_specs, check_vma=False)
```

```python
import functools
import math

import jax
import jax.numpy as jnp
from jax import lax
from jax.experimental import pallas as pl
from jax.experimental.pallas import tpu as pltpu
from jax.sharding import Mesh
from jax.sharding import PartitionSpec as P

HD = 128
GROUP = 16
PAGE = 16
SPAN = 64
NZ = 8
CHUNKS = 2
ROWS = SPAN // CHUNKS
WIDTH = GROUP * HD
LOG2E = 1.4426950408889634
HIDDEN = -1e30
KEYS = 640
F32 = jnp.float32
BF16 = jnp.bfloat16


def shift(block, axis, distance):
    n = lax.axis_size(axis)
    return lax.ppermute(block, axis, [(i, (i + distance) % n) for i in range(n)])


def flip(block, axis):
    return shift(block, axis, 1)


def flip_both(block):
    return lax.ppermute(block, ("xlo", "core"), [(i, 3 - i) for i in range(4)])


def outward(block):
    route = []
    for z in range(NZ):
        route.append((2 * z, 2 * ((z + 1) % NZ)))
        route.append((2 * z + 1, 2 * ((z - 1) % NZ) + 1))
    return lax.ppermute(block, ("z", "core"), route)


def pack_kernel(k, v, ck, cv, out):
    out[0:128] = k[...].T
    out[128:256] = v[...]
    out[256:288] = ck[...]
    out[288:320] = cv[...]


def pack(k, v, ck, cv):
    return pl.pallas_call(
        pack_kernel,
        out_shape=jax.ShapeDtypeStruct((320, HD), BF16),
        name="pack",
    )(k, v, ck, cv)


def attention_kernel(meta, order, length, q_own, q_got, *rest, slots, scale, first, last, chunk):
    n_refs = 1 + max(part[0] for slot in slots for part in slot)
    kv_refs, rest = rest[:n_refs], rest[n_refs:]
    if not first:
        top_in, acc_in, rest = rest[0], rest[1], rest[2:]
    tile = pl.program_id(0)
    span = tile % 2
    xlo, z, core = meta[0], meta[1], meta[2]
    first_row = (chunk if last else tile // 2) * ROWS
    lane128 = lax.broadcasted_iota(jnp.int32, (1, 128), 1)

    def source_of(side, part, distance):
        sign = jnp.where((core + side) % 2 == 0, -1, 1)
        sz = (z + sign * distance + NZ) % NZ
        return ((xlo + part % 2) % 2) * 16 + sz * 2 + (core + part // 2 + side) % 2

    own_place = order[2 * (xlo * 16 + z * 2 + core) + xlo]
    got_place = order[2 * ((1 - xlo) * 16 + z * 2 + core) + xlo]
    mine = span == xlo
    my_place = jnp.where(mine, own_place, got_place)
    q_rows = jnp.where(mine, q_own[...], q_got[...])
    halves = 2
    half_heads = GROUP // halves
    half_rows = half_heads * ROWS
    q_tiles = [
        jnp.concatenate([q_rows[:, i * HD : (i + 1) * HD] for i in range(h * half_heads, (h + 1) * half_heads)], axis=0)
        for h in range(halves)
    ]
    tops = [None if first else top_in[h * half_rows : (h + 1) * half_rows] for h in range(halves)]
    accs = [None if first else acc_in[h * half_rows : (h + 1) * half_rows] for h in range(halves)]

    for slot in slots:
        parts = [kv_refs[ref].at[place] for ref, place, *_ in slot]
        keys = jnp.concatenate(
            [p[0:128] for p in parts] + [jnp.concatenate([p[256:288] for p in parts], axis=0).T], axis=1
        )
        values = jnp.concatenate([p[128:256] for p in parts] + [p[288:320] for p in parts], axis=0)
        values = jnp.concatenate([values, jnp.ones((KEYS, HD), BF16)], axis=1)
        places = []
        cache_slot = lane128 % 32
        for i, (_, _, side, part, distance) in enumerate(slot):
            ctx = source_of(side, part, distance)
            places.append(jnp.where(lane128 < SPAN, order[2 * ctx], order[2 * ctx + 1]))
            cache_slot = jnp.where(lane128 // 32 == i, cache_slot + ctx * 32, cache_slot)
        places.append(jnp.where(cache_slot < length[0], -1, 64))
        places = jnp.concatenate(places, axis=1)
        bias = jnp.where(places < my_place, 0.0, HIDDEN)
        has_diagonal = slot[0][4] == 0
        if has_diagonal:
            lane = lax.broadcasted_iota(jnp.int32, (1, KEYS), 1) % SPAN
            diagonal = jnp.where(places == my_place, lane, 1000)
            row = lax.broadcasted_iota(jnp.int32, (half_rows, 1), 0) % ROWS + first_row
        for h in range(halves):
            s = jnp.dot(q_tiles[h], keys, preferred_element_type=F32) * scale
            if has_diagonal:
                s = jnp.where(diagonal <= row, s, s + bias)
            else:
                s = s + bias
            peak = functools.reduce(jnp.maximum, [s[:, i * 128 : (i + 1) * 128] for i in range(5)])
            peak = jnp.broadcast_to(jnp.max(peak, axis=1, keepdims=True), (half_rows, 128))
            top = peak if tops[h] is None else jnp.maximum(tops[h], peak)
            weights = jnp.concatenate(
                [jnp.exp2(s[:, i * 128 : (i + 1) * 128] - top) for i in range(5)], axis=1
            ).astype(BF16)
            added = jnp.dot(weights, values, preferred_element_type=F32)
            if accs[h] is None:
                accs[h] = added
            else:
                factor = jnp.exp2(tops[h] - top)
                accs[h] = accs[h] * jnp.concatenate([factor, factor], axis=1) + added
            tops[h] = top

    if last:
        (out,) = rest
        for h in range(halves):
            result = (accs[h][:, :HD] / accs[h][:, HD:]).astype(BF16)
            for i in range(half_heads):
                col = (h * half_heads + i) * HD
                out[0, :, col : col + HD] = result[i * ROWS : (i + 1) * ROWS]
    else:
        top_out, acc_out = rest
        for h in range(halves):
            top_out[h * half_rows : (h + 1) * half_rows] = tops[h]
            acc_out[h * half_rows : (h + 1) * half_rows] = accs[h]


def attention(meta, order, length, q_own, q_got, kv_blocks, slots, state, chunk=None):
    last, first = chunk is not None, state is None
    tile_rows = ROWS * GROUP
    base = 2 * chunk if last else 0
    q_spec = pl.BlockSpec((ROWS, WIDTH), lambda step, *_: ((base + step) // 2, 0))
    whole = [pl.BlockSpec(b.shape, lambda step, *_: (0, 0, 0)) for b in kv_blocks]
    state_shapes = [jax.ShapeDtypeStruct((2 * CHUNKS * tile_rows, w), F32) for w in (HD, 2 * HD)]
    in_state = [pl.BlockSpec((tile_rows, w), lambda step, *_: (base + step, 0)) for w in (HD, 2 * HD)]
    if last:
        out_shape = jax.ShapeDtypeStruct((2, ROWS, WIDTH), BF16)
        out_specs = pl.BlockSpec((1, ROWS, WIDTH), lambda step, *_: (step, 0, 0))
    else:
        out_shape, out_specs = state_shapes, [pl.BlockSpec((tile_rows, w), lambda step, *_: (step, 0)) for w in (HD, 2 * HD)]
    tiles = 2 if last else 2 * CHUNKS
    work = tiles * tile_rows * KEYS * len(slots)
    return pl.pallas_call(
        functools.partial(attention_kernel, slots=slots, scale=LOG2E / math.sqrt(HD), first=first, last=last, chunk=chunk),
        out_shape=out_shape,
        grid_spec=pltpu.PrefetchScalarGridSpec(
            num_scalar_prefetch=3,
            grid=(tiles,),
            in_specs=[q_spec, q_spec] + whole + ([] if first else in_state),
            out_specs=out_specs,
        ),
        compiler_params=pltpu.CompilerParams(vmem_limit_bytes=20 * 1024 * 1024),
        cost_estimate=pl.CostEstimate(flops=work * 4 * 256, bytes_accessed=4 * 2**20, transcendentals=work),
        name="attention",
    )(meta, order, length, q_own, q_got, *kv_blocks, *([] if first else state))


def parts_of(ref, side, distance, count=4, offset=0):
    return [(ref, i, side, offset + i, distance) for i in range(count)]


def project_kernel(meta, *refs):
    a_refs, w_refs, outs, rows = refs[:9], refs[9:13], refs[13:21], refs[21]
    z, y, xhi = meta[1], meta[2], meta[3]

    def bring(source, s, distance):
        place = (z + distance + NZ) % NZ
        part = (2 * s + place // 4 - y + 4) % 4
        inner = 2 * ((place // 2 + xhi) % 2) + place % 2
        rows[pl.ds(pl.multiple_of((part * 4 + inner) * ROWS, ROWS), ROWS)] = source[...]

    for s in range(2):
        bring(a_refs[0].at[s], s, 0)
        for d in range(1, 4):
            bring(a_refs[d].at[s], s, -d)
            bring(a_refs[3 + d].at[s], s, d)
    bring(a_refs[7].at[0], 0, 4)
    bring(a_refs[8].at[0], 1, 4)
    for i in range(4):
        total = jnp.dot(rows[...], w_refs[i][...], preferred_element_type=F32).astype(BF16)
        for k in range(8):
            outs[k][:, 512 * i : 512 * (i + 1)] = total[2 * k * ROWS : 2 * (k + 1) * ROWS]


SMEM_SPEC = pl.BlockSpec(memory_space=pltpu.SMEM)
VMEM_SPEC = pl.BlockSpec(memory_space=pltpu.VMEM)


def project(meta, blocks, weights):
    return pl.pallas_call(
        project_kernel,
        out_shape=[jax.ShapeDtypeStruct((2 * ROWS, 2048), BF16)] * 8,
        in_specs=[SMEM_SPEC] + [VMEM_SPEC] * 13,
        out_specs=[VMEM_SPEC] * 8,
        scratch_shapes=[pltpu.VMEM((16 * ROWS, WIDTH), BF16)],
        compiler_params=pltpu.CompilerParams(vmem_limit_bytes=12 * 1024 * 1024),
        cost_estimate=pl.CostEstimate(flops=2 * 16 * ROWS * 2048 * 2048, bytes_accessed=16 * 2**20, transcendentals=0),
        name="project",
    )(meta, *blocks, *weights)


def add2(x, y):
    return (x.astype(F32) + y.astype(F32)).astype(BF16)


def last_sum_kernel(x, y, z, u, *outs):
    total = x[...].astype(F32) + y[...].astype(F32) + z[...].astype(F32) + u[...].astype(F32)
    for i, out in enumerate(outs):
        out[...] = total[:, 512 * i : 512 * (i + 1)].astype(BF16)


def last_sum(*terms):
    return pl.pallas_call(
        last_sum_kernel,
        out_shape=[jax.ShapeDtypeStruct((2 * ROWS, 512), BF16)] * 4,
        in_specs=[VMEM_SPEC] * 4,
        out_specs=[VMEM_SPEC] * 4,
        compiler_params=pltpu.CompilerParams(vmem_limit_bytes=4 * 1024 * 1024),
        name="last_sum",
    )(*terms)


def assemble_kernel(meta, *refs):
    pieces, out = refs[:-1], refs[-1]
    xlo, core = meta[0], meta[1]
    for j in range(CHUNKS):
        for i in range(4):
            from_core = (core + i % 2) % 2
            from_xlo = (xlo + i // 2) % 2
            for zi in range(2):
                row = (zi * 2 + from_core) * 128 + from_xlo * SPAN + j * ROWS
                out[pl.ds(pl.multiple_of(row, 32), ROWS)] = pieces[4 * j + i][zi * ROWS : (zi + 1) * ROWS]


def assemble(meta, pieces):
    return pl.pallas_call(
        assemble_kernel,
        out_shape=jax.ShapeDtypeStruct((512, 512), BF16),
        in_specs=[SMEM_SPEC] + [VMEM_SPEC] * (4 * CHUNKS),
        out_specs=VMEM_SPEC,
        compiler_params=pltpu.CompilerParams(vmem_limit_bytes=4 * 1024 * 1024),
        name="assemble",
    )(meta, *pieces)


def after(value, *others):
    return lax.optimization_barrier((value, *others))[0]


def shards(
    queries, seg_keys, seg_values, cache_keys, cache_values, span_order, cache_length, out_weight
):
    xlo, z, core = lax.axis_index("xlo"), lax.axis_index("z"), lax.axis_index("core")
    y, xhi = lax.axis_index("y"), lax.axis_index("xhi")

    packed = pack(seg_keys, seg_values, cache_keys, cache_values)
    kv_core, kv_xlo, kv_both = flip(packed, "core"), flip(packed, "xlo"), flip_both(packed)
    give = lax.dynamic_slice_in_dim(queries, (1 - xlo) * SPAN, SPAN, 0)
    q_own = lax.dynamic_slice_in_dim(queries, xlo * SPAN, SPAN, 0)
    q_got = flip(after(give, kv_xlo, kv_both), "xlo")
    kv_own = jnp.stack([packed, kv_xlo, kv_core, kv_both])
    meta = jnp.stack([xlo, z, core])
    attend = functools.partial(attention, meta, span_order, cache_length, q_own, q_got)
    ring1 = outward(kv_own)
    cross1 = flip(ring1, "core")
    w_xlo = flip(after(out_weight, ring1, q_got), "xlo")
    ring2 = outward(ring1)
    cross2 = flip(ring2, "core")
    state = attend([kv_own, ring1], [parts_of(0, 0, 0), parts_of(1, 0, 1)], None)
    ring3 = outward(after(ring2, state[0]))
    cross3 = flip(ring3, "core")
    state = attend([ring2, cross1], [parts_of(0, 0, 2), parts_of(1, 1, 1)], state)
    ring4 = outward(after(ring3[:2], state[0]))
    cross4 = flip(ring4, "core")
    state = attend([ring3, cross2], [parts_of(0, 0, 3), parts_of(1, 1, 2)], state)
    w_core = flip(after(out_weight, cross4), "core")
    far_slots = [parts_of(0, 1, 3), parts_of(1, 0, 4, 2) + parts_of(2, 1, 4, 2)]
    attended = [attend([cross3, ring4, cross4], far_slots, state, 0)]
    state = (after(state[0], attended[0]), state[1])
    attended.append(attend([cross3, ring4, cross4], far_slots, state, 1))

    blocks = []
    for j in range(CHUNKS):
        ahead, behind = [], []
        up = down = attended[j]
        for d in range(3):
            up, down = shift(up, "z", 1), shift(down, "z", -1)
            behind.append(up)
            ahead.append(down)
            if j == 0 and d == 0:
                up, down = after(up, *attended), after(down, *attended)
        far = [shift(up[:1], "z", 1), shift(down[1:], "z", -1)]
        blocks.append([attended[j], *behind, *ahead, *far])
    w_both = flip(after(w_xlo, blocks[0][3], blocks[0][6], blocks[1][2], blocks[1][5]), "core")
    weights = [out_weight, w_core, w_xlo, w_both]

    meta_project = jnp.stack([xlo, z, y, xhi])
    pieces = []
    before = ()
    for j in range(CHUNKS):
        own_a, own_b, p1a, p1b, p2a, p2b, p3a, p3b = project(meta_project, blocks[j], weights)
        p2a, p2b = after(p2a, *before), after(p2b, *before)
        far_a, far_b = shift(p2a, "y", 1), shift(p2b, "y", -1)
        in1b, in3a = shift(after(p1b, *before), "y", 1), shift(after(p3a, *before), "y", -1)
        sum_a, sum_b = add2(p1a, far_a), add2(p3b, far_b)
        before = (sum_a, sum_b)
        in1a, in3b = shift(sum_a, "y", 1), shift(sum_b, "y", -1)
        give_b = (own_b.astype(F32) + in1b.astype(F32) + in3b.astype(F32)).astype(BF16)
        got_a = flip(give_b, "xhi")
        mine, to_core, to_xlo, to_both = last_sum(own_a, in1a, in3a, got_a)
        pieces += [mine, flip(to_core, "core"), flip(to_xlo, "xlo"), flip_both(to_both)]
    mixed = assemble(jnp.stack([xlo, core]), pieces)
    paged_keys = seg_keys.reshape(seg_keys.shape[0] // PAGE, PAGE, seg_keys.shape[1])
    return (mixed, jnp.min(paged_keys, axis=1), jnp.max(paged_keys, axis=1))


def solution(mesh):
    split = Mesh(mesh.devices.reshape(2, NZ, 2, 4, 2), ("xlo", "z", "core", "y", "xhi"))
    ctx, head = ("xlo", "z", "core"), ("y", "xhi")
    in_specs = (
        P(ctx, head),
        P(ctx, head),
        P(ctx, head),
        P(ctx, head),
        P(ctx, head),
        P(),
        P(),
        P(head, ctx),
    )
    out_specs = (P(head, ctx), P(ctx, head), P(ctx, head))
    return jax.shard_map(shards, mesh=split, in_specs=in_specs, out_specs=out_specs, check_vma=False)
```

```python
import functools
import math

import jax
import jax.numpy as jnp
from jax import lax
from jax.experimental import pallas as pl
from jax.experimental.pallas import tpu as pltpu
from jax.sharding import Mesh
from jax.sharding import PartitionSpec as P

HD = 128
GROUP = 16
PAGE = 16
SPAN = 64
NZ = 8
CHUNKS = 2
ROWS = SPAN // CHUNKS
WIDTH = GROUP * HD
LOG2E = 1.4426950408889634
HIDDEN = -1e30
KEYS = 640
HALVES = 2
F32 = jnp.float32
BF16 = jnp.bfloat16


def shift(block, axis, distance):
    n = lax.axis_size(axis)
    return lax.ppermute(block, axis, [(i, (i + distance) % n) for i in range(n)])


def flip(block, axis):
    return shift(block, axis, 1)


def flip_both(block):
    return lax.ppermute(block, ("xlo", "core"), [(i, 3 - i) for i in range(4)])


def outward(block):
    route = []
    for z in range(NZ):
        route.append((2 * z, 2 * ((z + 1) % NZ)))
        route.append((2 * z + 1, 2 * ((z - 1) % NZ) + 1))
    return lax.ppermute(block, ("z", "core"), route)


def pack_kernel(k, v, ck, cv, out):
    out[0:128] = k[...].T
    out[128:256] = v[...]
    out[256:288] = ck[...]
    out[288:320] = cv[...]


def pack(k, v, ck, cv):
    return pl.pallas_call(
        pack_kernel,
        out_shape=jax.ShapeDtypeStruct((320, HD), BF16),
        name="pack",
    )(k, v, ck, cv)


def attention_kernel(meta, order, length, q_own, q_got, *rest, slots, scale, first, last, chunk):
    n_refs = 1 + max(part[0] for slot in slots for part in slot)
    kv_refs, rest = rest[:n_refs], rest[n_refs:]
    if not first:
        top_in, acc_in, rest = rest[0], rest[1], rest[2:]
    tile = pl.program_id(0)
    span = tile % 2
    xlo, z, core = meta[0], meta[1], meta[2]
    first_row = (chunk if last else tile // 2) * ROWS
    lane128 = lax.broadcasted_iota(jnp.int32, (1, 128), 1)

    def source_of(side, part, distance):
        sign = jnp.where((core + side) % 2 == 0, -1, 1)
        sz = (z + sign * distance + NZ) % NZ
        return ((xlo + part % 2) % 2) * 16 + sz * 2 + (core + part // 2 + side) % 2

    own_place = order[2 * (xlo * 16 + z * 2 + core) + xlo]
    got_place = order[2 * ((1 - xlo) * 16 + z * 2 + core) + xlo]
    mine = span == xlo
    my_place = jnp.where(mine, own_place, got_place)
    q_rows = jnp.where(mine, q_own[...], q_got[...])
    half_heads = GROUP // HALVES
    half_rows = half_heads * ROWS
    q_tiles = [
        jnp.concatenate([q_rows[:, i * HD : (i + 1) * HD] for i in range(h * half_heads, (h + 1) * half_heads)], axis=0)
        for h in range(HALVES)
    ]

    keys, values, biases, diagonal = [], [], [], None
    for slot in slots:
        parts = [kv_refs[ref].at[place] for ref, place, *_ in slot]
        block = jnp.concatenate(
            [p[0:128] for p in parts] + [jnp.concatenate([p[256:288] for p in parts], axis=0).T], axis=1
        )
        block_values = jnp.concatenate([p[128:256] for p in parts] + [p[288:320] for p in parts], axis=0)
        values.append(jnp.concatenate([block_values, jnp.ones((KEYS, HD), BF16)], axis=1))
        places = []
        cache_slot = lane128 % 32
        for i, (_, _, side, part, distance) in enumerate(slot):
            ctx = source_of(side, part, distance)
            places.append(jnp.where(lane128 < SPAN, order[2 * ctx], order[2 * ctx + 1]))
            cache_slot = jnp.where(lane128 // 32 == i, cache_slot + ctx * 32, cache_slot)
        places.append(jnp.where(cache_slot < length[0], -1, 64))
        places = jnp.concatenate(places, axis=1)
        has_diagonal = slot[0][4] == 0
        biases.append(jnp.where(places < my_place, 0.0, HIDDEN))
        if has_diagonal:
            lane = lax.broadcasted_iota(jnp.int32, (1, KEYS), 1) % SPAN
            diagonal = jnp.where(places == my_place, lane, 1000)
        keys.append(block)
    row = lax.broadcasted_iota(jnp.int32, (half_rows, 1), 0) % ROWS + first_row

    def scores_of(h, i):
        s = jnp.dot(q_tiles[h], keys[i], preferred_element_type=F32) * scale
        if slots[i][0][4] == 0:
            return jnp.where(diagonal <= row, s, s + biases[i])
        return s + biases[i]

    tops, accs = [], []
    for h in range(HALVES):
        at = slice(h * half_rows, (h + 1) * half_rows)
        scores = [scores_of(h, i) for i in range(len(slots))]
        pieces = [s[:, i * 128 : (i + 1) * 128] for s in scores for i in range(5)]
        peak = functools.reduce(jnp.maximum, pieces)
        top = jnp.broadcast_to(jnp.max(peak, axis=1, keepdims=True), (half_rows, 128))
        if not first:
            top = jnp.maximum(top_in[at], top)
            factor = jnp.exp2(top_in[at] - top)
            acc = acc_in[at] * jnp.concatenate([factor, factor], axis=1)
        else:
            acc = None
        for i in range(len(slots)):
            weights = jnp.concatenate(
                [jnp.exp2(p - top) for p in pieces[5 * i : 5 * i + 5]], axis=1
            ).astype(BF16)
            added = jnp.dot(weights, values[i], preferred_element_type=F32)
            acc = added if acc is None else acc + added
        tops.append(top)
        accs.append(acc)

    if last:
        (out,) = rest
        for h in range(HALVES):
            result = (accs[h][:, :HD] / accs[h][:, HD:]).astype(BF16)
            for i in range(half_heads):
                col = (h * half_heads + i) * HD
                out[0, :, col : col + HD] = result[i * ROWS : (i + 1) * ROWS]
    else:
        top_out, acc_out = rest
        for h in range(HALVES):
            top_out[h * half_rows : (h + 1) * half_rows] = tops[h]
            acc_out[h * half_rows : (h + 1) * half_rows] = accs[h]


def attention(meta, order, length, q_own, q_got, kv_blocks, slots, state, chunk=None):
    last, first = chunk is not None, state is None
    tile_rows = ROWS * GROUP
    base = 2 * chunk if last else 0
    q_spec = pl.BlockSpec((ROWS, WIDTH), lambda step, *_: ((base + step) // 2, 0))
    whole = [pl.BlockSpec(b.shape, lambda step, *_: (0, 0, 0)) for b in kv_blocks]
    state_shapes = [jax.ShapeDtypeStruct((2 * CHUNKS * tile_rows, w), F32) for w in (HD, 2 * HD)]
    in_state = [pl.BlockSpec((tile_rows, w), lambda step, *_: (base + step, 0)) for w in (HD, 2 * HD)]
    if last:
        out_shape = jax.ShapeDtypeStruct((2, ROWS, WIDTH), BF16)
        out_specs = pl.BlockSpec((1, ROWS, WIDTH), lambda step, *_: (step, 0, 0))
    else:
        out_shape, out_specs = state_shapes, [pl.BlockSpec((tile_rows, w), lambda step, *_: (step, 0)) for w in (HD, 2 * HD)]
    tiles = 2 if last else 2 * CHUNKS
    work = tiles * tile_rows * KEYS * len(slots)
    return pl.pallas_call(
        functools.partial(attention_kernel, slots=slots, scale=LOG2E / math.sqrt(HD), first=first, last=last, chunk=chunk),
        out_shape=out_shape,
        grid_spec=pltpu.PrefetchScalarGridSpec(
            num_scalar_prefetch=3,
            grid=(tiles,),
            in_specs=[q_spec, q_spec] + whole + ([] if first else in_state),
            out_specs=out_specs,
        ),
        compiler_params=pltpu.CompilerParams(vmem_limit_bytes=20 * 1024 * 1024),
        cost_estimate=pl.CostEstimate(flops=work * 32, bytes_accessed=2**18, transcendentals=work // 64),
        name="attention",
    )(meta, order, length, q_own, q_got, *kv_blocks, *([] if first else state))


def parts_of(ref, side, distance, count=4, offset=0):
    return [(ref, i, side, offset + i, distance) for i in range(count)]


def slot_of(meta, s, distance):
    z, y, xhi = meta[1], meta[2], meta[3]
    place = (z + distance + NZ) % NZ
    part = (2 * s + place // 4 - y + 4) % 4
    other = (place // 2 + xhi) % 2
    index = 2 * part + other
    group = jnp.int32(7)
    for position, key in enumerate((4, 3, 5, 6, 0, 1, 2)):
        group = jnp.where(index == key, position, group)
    return 2 * group + place % 2


def place_kernel(meta, *refs, distances):
    n = len(distances)
    sources, out, sem = refs[:n], refs[-2], refs[-1]
    copies = []
    for source, distance in zip(sources, distances):
        for s in range(2):
            row = slot_of(meta, s, distance) * ROWS
            copies.append(
                pltpu.make_async_copy(
                    source.at[s], out.at[pl.ds(pl.multiple_of(row, ROWS), ROWS)], sem.at[len(copies)]
                )
            )
    for c in copies:
        c.start()
    for c in copies:
        c.wait()


def place_rows(meta, sources, distances, rows=None):
    fresh = rows is None
    n = len(sources)
    return pl.pallas_call(
        functools.partial(place_kernel, distances=distances),
        out_shape=jax.ShapeDtypeStruct((16 * ROWS, WIDTH), BF16),
        in_specs=[SMEM_SPEC] + [VMEM_SPEC] * n + ([] if fresh else [pl.BlockSpec(memory_space=pl.ANY)]),
        out_specs=pl.BlockSpec(memory_space=pl.ANY),
        scratch_shapes=[pltpu.SemaphoreType.DMA((2 * n,))],
        input_output_aliases={} if fresh else {n + 1: 0},
        compiler_params=pltpu.CompilerParams(vmem_limit_bytes=4 * 1024 * 1024),
        name="place_rows",
    )(meta, *sources, *([] if fresh else [rows]))


SMEM_SPEC = pl.BlockSpec(memory_space=pltpu.SMEM)
VMEM_SPEC = pl.BlockSpec(memory_space=pltpu.VMEM)


def project_kernel(meta, held, *refs, late, group):
    n = len(late)
    sources, w_refs, outs, rows, sem = refs[:n], refs[n : n + 4], refs[n + 4 : -2], refs[-2], refs[-1]
    mine = pl.ds(group * 8 * ROWS, 8 * ROWS)
    copy = pltpu.make_async_copy(held.at[mine], rows.at[mine], sem)
    copy.start()
    copy.wait()
    for source, (distance, halves) in zip(sources, late):
        for i, s in enumerate(halves):
            row = slot_of(meta, s, distance) * ROWS
            rows[pl.ds(pl.multiple_of(row, ROWS), ROWS)] = source[i]
    for i in range(4):
        total = jnp.dot(rows[mine], w_refs[i][...], preferred_element_type=F32).astype(BF16)
        size = 8 * ROWS // len(outs)
        for k, out in enumerate(outs):
            out[:, 512 * i : 512 * (i + 1)] = total[k * size : (k + 1) * size]


def project(meta, held, late, distances, weights, group):
    count = (2, 4)[group]
    return pl.pallas_call(
        functools.partial(project_kernel, late=distances, group=group),
        out_shape=[jax.ShapeDtypeStruct((8 * ROWS // count, 2048), BF16)] * count,
        in_specs=[SMEM_SPEC, pl.BlockSpec(memory_space=pl.ANY)] + [VMEM_SPEC] * (len(late) + 4),
        out_specs=[VMEM_SPEC] * count,
        scratch_shapes=[pltpu.VMEM((16 * ROWS, WIDTH), BF16), pltpu.SemaphoreType.DMA],
        compiler_params=pltpu.CompilerParams(vmem_limit_bytes=12 * 1024 * 1024),
        cost_estimate=pl.CostEstimate(flops=2 * ROWS * 2048 * 2048, bytes_accessed=1 * 2**20, transcendentals=0),
        name="project",
    )(meta, held, *late, *weights)


def add2(x, y):
    return (x.astype(F32) + y.astype(F32)).astype(BF16)


def last_sum_kernel(x, y, z, u, *outs):
    total = x[...].astype(F32) + y[...].astype(F32) + z[2 * ROWS :].astype(F32) + u[...].astype(F32)
    for i, out in enumerate(outs):
        out[...] = total[:, 512 * i : 512 * (i + 1)].astype(BF16)


def last_sum(*terms):
    return pl.pallas_call(
        last_sum_kernel,
        out_shape=[jax.ShapeDtypeStruct((2 * ROWS, 512), BF16)] * 4,
        in_specs=[VMEM_SPEC] * 4,
        out_specs=[VMEM_SPEC] * 4,
        compiler_params=pltpu.CompilerParams(vmem_limit_bytes=4 * 1024 * 1024),
        name="last_sum",
    )(*terms)


def assemble_kernel(meta, *refs):
    pieces, out = refs[:-1], refs[-1]
    xlo, core = meta[0], meta[1]
    for j in range(CHUNKS):
        for i in range(4):
            from_core = (core + i % 2) % 2
            from_xlo = (xlo + i // 2) % 2
            for zi in range(2):
                row = (zi * 2 + from_core) * 128 + from_xlo * SPAN + j * ROWS
                out[pl.ds(pl.multiple_of(row, 32), ROWS)] = pieces[4 * j + i][zi * ROWS : (zi + 1) * ROWS]


def assemble(meta, pieces):
    return pl.pallas_call(
        assemble_kernel,
        out_shape=jax.ShapeDtypeStruct((512, 512), BF16),
        in_specs=[SMEM_SPEC] + [VMEM_SPEC] * (4 * CHUNKS),
        out_specs=VMEM_SPEC,
        compiler_params=pltpu.CompilerParams(vmem_limit_bytes=4 * 1024 * 1024),
        name="assemble",
    )(meta, *pieces)


def after(value, *others):
    return lax.optimization_barrier((value, *others))[0]


def shards(
    queries, seg_keys, seg_values, cache_keys, cache_values, span_order, cache_length, out_weight
):
    xlo, z, core = lax.axis_index("xlo"), lax.axis_index("z"), lax.axis_index("core")
    y, xhi = lax.axis_index("y"), lax.axis_index("xhi")

    packed = pack(seg_keys, seg_values, cache_keys, cache_values)
    kv_core, kv_xlo, kv_both = flip(packed, "core"), flip(packed, "xlo"), flip_both(packed)
    give = lax.dynamic_slice_in_dim(queries, (1 - xlo) * SPAN, SPAN, 0)
    q_own = lax.dynamic_slice_in_dim(queries, xlo * SPAN, SPAN, 0)
    q_got = flip(after(give, packed), "xlo")
    kv_own = jnp.stack([packed, kv_xlo, kv_core, kv_both])
    meta = jnp.stack([xlo, z, core])
    attend = functools.partial(attention, meta, span_order, cache_length, q_own, q_got)
    ring1 = outward(kv_own)
    cross1 = flip(ring1, "core")
    w_gated = after(out_weight, ring1, q_got)
    w_xlo, w_core = flip(w_gated, "xlo"), flip(w_gated, "core")
    ring2 = outward(ring1)
    cross2 = flip(ring2, "core")
    state = attend([kv_own, ring1], [parts_of(0, 0, 0), parts_of(1, 0, 1)], None)
    ring3 = outward(after(ring2, state[0]))
    cross3 = flip(ring3, "core")
    state = attend([ring2, cross1], [parts_of(0, 0, 2), parts_of(1, 1, 1)], state)
    ring4 = outward(after(ring3[:2], state[0], w_core))
    cross4 = flip(ring4, "core")
    state = attend([ring3, cross2], [parts_of(0, 0, 3), parts_of(1, 1, 2)], state)
    far_slots = [parts_of(0, 1, 3), parts_of(1, 0, 4, 2) + parts_of(2, 1, 4, 2)]
    attended = [attend([cross3, ring4, cross4], far_slots, state, 0)]
    state = (after(state[0], attended[0]), state[1])
    attended.append(attend([cross3, ring4, cross4], far_slots, state, 1))

    meta_project = jnp.stack([xlo, z, y, xhi])

    def both_ways(up, down, *others):
        return shift(after(up, *others), "z", 1), shift(after(down, *others), "z", -1)

    def place_near(own, up, down):
        return place_rows(meta_project, [own, up, down], (0, -1, 1))

    def place_far(rows, up, down):
        return place_rows(meta_project, [up, down], (-2, 2), rows)

    distances = ((-3, (0, 1)), (3, (0, 1)), (4, (0,)), (4, (1,)))
    first, second = attended
    a1 = both_ways(first, first)
    near = place_near(first, *a1)
    a2 = both_ways(*a1, second)
    b1 = both_ways(second, second, *a2)
    a3 = both_ways(*a2, near)
    held_a = place_far(near, *a2)
    w_both = flip(after(w_xlo, *a3, *b1), "core")
    weights = [out_weight, w_core, w_xlo, w_both]
    a4 = both_ways(a3[0][:1], a3[1][1:], held_a, *b1)
    near = place_near(second, *b1)
    b2 = both_ways(*b1, *a3)
    sends_a = project(meta_project, held_a, [*a3, *a4], distances, weights, 0)
    b3 = both_ways(*b2, near, *a4)
    held_b = place_far(near, *b2)
    rest_a = project(meta_project, held_a, [*a3, *a4], distances, weights, 1)
    b4 = both_ways(b3[0][:1], b3[1][1:], held_b, sends_a[0])
    sends_b = project(meta_project, held_b, [*b3, *b4], distances, weights, 0)
    rest_b = project(meta_project, held_b, [*b3, *b4], distances, weights, 1)

    pieces = []
    others = ()
    for (plus, minus), (own_a, own_b, p1a, p3b) in ((sends_a, rest_a), (sends_b, rest_b)):
        plus, minus = shift(after(plus, *others), "y", 1), shift(after(minus, *others), "y", -1)
        sum_a, sum_b = add2(p1a, plus[: 2 * ROWS]), add2(p3b, minus[: 2 * ROWS])
        others = (sum_a, sum_b)
        in1a, in3b = shift(sum_a, "y", 1), shift(sum_b, "y", -1)
        give_b = (own_b.astype(F32) + plus[2 * ROWS :].astype(F32) + in3b.astype(F32)).astype(BF16)
        got_a = flip(give_b, "xhi")
        mine, to_core, to_xlo, to_both = last_sum(own_a, in1a, minus, got_a)
        pieces += [mine, flip(to_core, "core"), flip(to_xlo, "xlo"), flip_both(to_both)]
    mixed = assemble(jnp.stack([xlo, core]), pieces)
    paged_keys = seg_keys.reshape(seg_keys.shape[0] // PAGE, PAGE, seg_keys.shape[1])
    return (mixed, jnp.min(paged_keys, axis=1), jnp.max(paged_keys, axis=1))


def solution(mesh):
    split = Mesh(mesh.devices.reshape(2, NZ, 2, 4, 2), ("xlo", "z", "core", "y", "xhi"))
    ctx, head = ("xlo", "z", "core"), ("y", "xhi")
    in_specs = (
        P(ctx, head),
        P(ctx, head),
        P(ctx, head),
        P(ctx, head),
        P(ctx, head),
        P(),
        P(),
        P(head, ctx),
    )
    out_specs = (P(head, ctx), P(ctx, head), P(ctx, head))
    return jax.shard_map(shards, mesh=split, in_specs=in_specs, out_specs=out_specs, check_vma=False)
```

```python
import functools
import math

import jax
import jax.numpy as jnp
from jax import lax
from jax.experimental import pallas as pl
from jax.experimental.pallas import tpu as pltpu
from jax.sharding import Mesh
from jax.sharding import PartitionSpec as P

HD = 128
GROUP = 16
PAGE = 16
SPAN = 64
NZ = 8
CHUNKS = 2
ROWS = SPAN // CHUNKS
WIDTH = GROUP * HD
LOG2E = 1.4426950408889634
HIDDEN = -1e30
KEYS = 640
HALVES = 2
F32 = jnp.float32
BF16 = jnp.bfloat16


def shift(block, axis, distance):
    n = lax.axis_size(axis)
    return lax.ppermute(block, axis, [(i, (i + distance) % n) for i in range(n)])


def flip(block, axis):
    return shift(block, axis, 1)


def flip_both(block):
    return lax.ppermute(block, ("xlo", "core"), [(i, 3 - i) for i in range(4)])


def outward(block):
    route = []
    for z in range(NZ):
        route.append((2 * z, 2 * ((z + 1) % NZ)))
        route.append((2 * z + 1, 2 * ((z - 1) % NZ) + 1))
    return lax.ppermute(block, ("z", "core"), route)


def pack_kernel(k, v, ck, cv, out):
    out[0:128] = k[...].T
    out[128:256] = v[...]
    out[256:288] = ck[...]
    out[288:320] = cv[...]


def pack(k, v, ck, cv):
    return pl.pallas_call(
        pack_kernel,
        out_shape=jax.ShapeDtypeStruct((320, HD), BF16),
        name="pack",
    )(k, v, ck, cv)


def attention_kernel(meta, order, length, q_own, q_got, *rest, slots, scale, first, last):
    n_refs = 1 + max(part[0] for slot in slots for part in slot)
    kv_refs, rest = rest[:n_refs], rest[n_refs:]
    if not first:
        top_in, acc_in, rest = rest[0], rest[1], rest[2:]
    tile = pl.program_id(0)
    span = tile % 2
    xlo, z, core = meta[0], meta[1], meta[2]
    first_row = tile // 2 * ROWS
    lane128 = lax.broadcasted_iota(jnp.int32, (1, 128), 1)

    def source_of(side, part, distance):
        sign = jnp.where((core + side) % 2 == 0, -1, 1)
        sz = (z + sign * distance + NZ) % NZ
        return ((xlo + part % 2) % 2) * 16 + sz * 2 + (core + part // 2 + side) % 2

    own_place = order[2 * (xlo * 16 + z * 2 + core) + xlo]
    got_place = order[2 * ((1 - xlo) * 16 + z * 2 + core) + xlo]
    mine = span == xlo
    my_place = jnp.where(mine, own_place, got_place)
    q_rows = jnp.where(mine, q_own[...], q_got[...])
    half_heads = GROUP // HALVES
    half_rows = half_heads * ROWS
    q_tiles = [
        jnp.concatenate([q_rows[:, i * HD : (i + 1) * HD] for i in range(h * half_heads, (h + 1) * half_heads)], axis=0)
        for h in range(HALVES)
    ]

    keys, values, biases, diagonal = [], [], [], None
    for slot in slots:
        parts = [kv_refs[ref].at[place] for ref, place, *_ in slot]
        block = jnp.concatenate(
            [p[0:128] for p in parts] + [jnp.concatenate([p[256:288] for p in parts], axis=0).T], axis=1
        )
        block_values = jnp.concatenate([p[128:256] for p in parts] + [p[288:320] for p in parts], axis=0)
        values.append(jnp.concatenate([block_values, jnp.ones((KEYS, HD), BF16)], axis=1))
        places = []
        cache_slot = lane128 % 32
        for i, (_, _, side, part, distance) in enumerate(slot):
            ctx = source_of(side, part, distance)
            places.append(jnp.where(lane128 < SPAN, order[2 * ctx], order[2 * ctx + 1]))
            cache_slot = jnp.where(lane128 // 32 == i, cache_slot + ctx * 32, cache_slot)
        places.append(jnp.where(cache_slot < length[0], -1, 64))
        places = jnp.concatenate(places, axis=1)
        has_diagonal = slot[0][4] == 0
        biases.append(jnp.where(places < my_place, 0.0, HIDDEN))
        if has_diagonal:
            lane = lax.broadcasted_iota(jnp.int32, (1, KEYS), 1) % SPAN
            diagonal = jnp.where(places == my_place, lane, 1000)
        keys.append(block)
    row = lax.broadcasted_iota(jnp.int32, (half_rows, 1), 0) % ROWS + first_row

    def scores_of(h, i):
        s = jnp.dot(q_tiles[h], keys[i], preferred_element_type=F32) * scale
        if slots[i][0][4] == 0:
            return jnp.where(diagonal <= row, s, s + biases[i])
        return s + biases[i]

    tops, accs = [], []
    for h in range(HALVES):
        at = slice(h * half_rows, (h + 1) * half_rows)
        scores = [scores_of(h, i) for i in range(len(slots))]
        pieces = [s[:, i * 128 : (i + 1) * 128] for s in scores for i in range(5)]
        peak = functools.reduce(jnp.maximum, pieces)
        top = jnp.broadcast_to(jnp.max(peak, axis=1, keepdims=True), (half_rows, 128))
        if not first:
            top = jnp.maximum(top_in[at], top)
            factor = jnp.exp2(top_in[at] - top)
            acc = acc_in[at] * jnp.concatenate([factor, factor], axis=1)
        else:
            acc = None
        for i in range(len(slots)):
            weights = jnp.concatenate(
                [jnp.exp2(p - top) for p in pieces[5 * i : 5 * i + 5]], axis=1
            ).astype(BF16)
            added = jnp.dot(weights, values[i], preferred_element_type=F32)
            acc = added if acc is None else acc + added
        tops.append(top)
        accs.append(acc)

    if last:
        for chunk in range(CHUNKS):

            @pl.when(tile // 2 == chunk)
            def _():
                for h in range(HALVES):
                    result = (accs[h][:, :HD] / accs[h][:, HD:]).astype(BF16)
                    for i in range(half_heads):
                        col = (h * half_heads + i) * HD
                        rest[chunk][0, :, col : col + HD] = result[i * ROWS : (i + 1) * ROWS]
    else:
        top_out, acc_out = rest
        for h in range(HALVES):
            top_out[h * half_rows : (h + 1) * half_rows] = tops[h]
            acc_out[h * half_rows : (h + 1) * half_rows] = accs[h]


def attention(meta, order, length, q_own, q_got, kv_blocks, slots, state, last=False):
    first = state is None
    tile_rows = ROWS * GROUP
    tiles = 2 * CHUNKS
    q_spec = pl.BlockSpec((ROWS, WIDTH), lambda step, *_: (step // 2, 0))
    whole = [pl.BlockSpec(b.shape, lambda step, *_: (0, 0, 0)) for b in kv_blocks]
    state_specs = [pl.BlockSpec((tile_rows, w), lambda step, *_: (step, 0)) for w in (HD, 2 * HD)]
    if last:

        def chunk_spec(chunk):
            return pl.BlockSpec((1, ROWS, WIDTH), lambda step, *_: (jnp.clip(step - 2 * chunk, 0, 1), 0, 0))

        out_shape = [jax.ShapeDtypeStruct((2, ROWS, WIDTH), BF16)] * CHUNKS
        out_specs = [chunk_spec(chunk) for chunk in range(CHUNKS)]
    else:
        out_shape = [jax.ShapeDtypeStruct((tiles * tile_rows, w), F32) for w in (HD, 2 * HD)]
        out_specs = state_specs
    work = tiles * tile_rows * KEYS * len(slots)
    return pl.pallas_call(
        functools.partial(attention_kernel, slots=slots, scale=LOG2E / math.sqrt(HD), first=first, last=last),
        out_shape=out_shape,
        grid_spec=pltpu.PrefetchScalarGridSpec(
            num_scalar_prefetch=3,
            grid=(tiles,),
            in_specs=[q_spec, q_spec] + whole + ([] if first else state_specs),
            out_specs=out_specs,
        ),
        compiler_params=pltpu.CompilerParams(vmem_limit_bytes=20 * 1024 * 1024),
        cost_estimate=pl.CostEstimate(flops=work * 32, bytes_accessed=2**18, transcendentals=work // 64),
        name="attention",
    )(meta, order, length, q_own, q_got, *kv_blocks, *([] if first else state))


def parts_of(ref, side, distance, count=4, offset=0):
    return [(ref, i, side, offset + i, distance) for i in range(count)]


def slot_of(meta, s, distance):
    z, y, xhi = meta[1], meta[2], meta[3]
    place = (z + distance + NZ) % NZ
    part = (2 * s + place // 4 - y + 4) % 4
    other = (place // 2 + xhi) % 2
    index = 2 * part + other
    group = jnp.int32(7)
    for position, key in enumerate((4, 3, 5, 6, 0, 1, 2)):
        group = jnp.where(index == key, position, group)
    return 2 * group + place % 2


def place_kernel(meta, *refs, distances):
    n = len(distances)
    sources, out, sem = refs[:n], refs[-2], refs[-1]
    copies = []
    for source, distance in zip(sources, distances):
        for s in range(2):
            row = slot_of(meta, s, distance) * ROWS
            copies.append(
                pltpu.make_async_copy(
                    source.at[s], out.at[pl.ds(pl.multiple_of(row, ROWS), ROWS)], sem.at[len(copies)]
                )
            )
    for c in copies:
        c.start()
    for c in copies:
        c.wait()


def place_rows(meta, sources, distances, rows=None):
    fresh = rows is None
    n = len(sources)
    return pl.pallas_call(
        functools.partial(place_kernel, distances=distances),
        out_shape=jax.ShapeDtypeStruct((16 * ROWS, WIDTH), BF16),
        in_specs=[SMEM_SPEC] + [VMEM_SPEC] * n + ([] if fresh else [pl.BlockSpec(memory_space=pl.ANY)]),
        out_specs=pl.BlockSpec(memory_space=pl.ANY),
        scratch_shapes=[pltpu.SemaphoreType.DMA((2 * n,))],
        input_output_aliases={} if fresh else {n + 1: 0},
        compiler_params=pltpu.CompilerParams(vmem_limit_bytes=4 * 1024 * 1024),
        name="place_rows",
    )(meta, *sources, *([] if fresh else [rows]))


SMEM_SPEC = pl.BlockSpec(memory_space=pltpu.SMEM)
VMEM_SPEC = pl.BlockSpec(memory_space=pltpu.VMEM)


def project_kernel(meta, held, *refs, late, group):
    n = len(late)
    sources, w_refs, outs, rows, sem = refs[:n], refs[n : n + 4], refs[n + 4 : -2], refs[-2], refs[-1]
    mine = pl.ds(group * 8 * ROWS, 8 * ROWS)
    copy = pltpu.make_async_copy(held.at[mine], rows.at[mine], sem)
    copy.start()
    copy.wait()
    for source, (distance, halves) in zip(sources, late):
        for i, s in enumerate(halves):
            row = slot_of(meta, s, distance) * ROWS
            rows[pl.ds(pl.multiple_of(row, ROWS), ROWS)] = source[i]
    for i in range(4):
        total = jnp.dot(rows[mine], w_refs[i][...], preferred_element_type=F32).astype(BF16)
        size = 8 * ROWS // len(outs)
        for k, out in enumerate(outs):
            out[:, 512 * i : 512 * (i + 1)] = total[k * size : (k + 1) * size]


def project(meta, held, late, distances, weights, group):
    count = (2, 4)[group]
    return pl.pallas_call(
        functools.partial(project_kernel, late=distances, group=group),
        out_shape=[jax.ShapeDtypeStruct((8 * ROWS // count, 2048), BF16)] * count,
        in_specs=[SMEM_SPEC, pl.BlockSpec(memory_space=pl.ANY)] + [VMEM_SPEC] * (len(late) + 4),
        out_specs=[VMEM_SPEC] * count,
        scratch_shapes=[pltpu.VMEM((16 * ROWS, WIDTH), BF16), pltpu.SemaphoreType.DMA],
        compiler_params=pltpu.CompilerParams(vmem_limit_bytes=12 * 1024 * 1024),
        cost_estimate=pl.CostEstimate(flops=64 * ROWS * 2048 * 2048, bytes_accessed=1 * 2**20, transcendentals=0),
        name="project",
    )(meta, held, *late, *weights)


def add2(x, y):
    return (x.astype(F32) + y.astype(F32)).astype(BF16)


def last_sum_kernel(x, y, z, u, *outs):
    total = x[...].astype(F32) + y[...].astype(F32) + z[2 * ROWS :].astype(F32) + u[...].astype(F32)
    for i, out in enumerate(outs):
        out[...] = total[:, 512 * i : 512 * (i + 1)].astype(BF16)


def last_sum(*terms):
    return pl.pallas_call(
        last_sum_kernel,
        out_shape=[jax.ShapeDtypeStruct((2 * ROWS, 512), BF16)] * 4,
        in_specs=[VMEM_SPEC] * 4,
        out_specs=[VMEM_SPEC] * 4,
        compiler_params=pltpu.CompilerParams(vmem_limit_bytes=4 * 1024 * 1024),
        name="last_sum",
    )(*terms)


def assemble_kernel(meta, *refs):
    pieces, out = refs[:-1], refs[-1]
    xlo, core = meta[0], meta[1]
    for j in range(CHUNKS):
        for i in range(4):
            from_core = (core + i % 2) % 2
            from_xlo = (xlo + i // 2) % 2
            for zi in range(2):
                row = (zi * 2 + from_core) * 128 + from_xlo * SPAN + j * ROWS
                out[pl.ds(pl.multiple_of(row, 32), ROWS)] = pieces[4 * j + i][zi * ROWS : (zi + 1) * ROWS]


def assemble(meta, pieces):
    return pl.pallas_call(
        assemble_kernel,
        out_shape=jax.ShapeDtypeStruct((512, 512), BF16),
        in_specs=[SMEM_SPEC] + [VMEM_SPEC] * (4 * CHUNKS),
        out_specs=VMEM_SPEC,
        compiler_params=pltpu.CompilerParams(vmem_limit_bytes=4 * 1024 * 1024),
        name="assemble",
    )(meta, *pieces)


def after(value, *others):
    return lax.optimization_barrier((value, *others))[0]


def shards(
    queries, seg_keys, seg_values, cache_keys, cache_values, span_order, cache_length, out_weight
):
    xlo, z, core = lax.axis_index("xlo"), lax.axis_index("z"), lax.axis_index("core")
    y, xhi = lax.axis_index("y"), lax.axis_index("xhi")

    packed = pack(seg_keys, seg_values, cache_keys, cache_values)
    kv_core, kv_xlo, kv_both = flip(packed, "core"), flip(packed, "xlo"), flip_both(packed)
    give = lax.dynamic_slice_in_dim(queries, (1 - xlo) * SPAN, SPAN, 0)
    q_own = lax.dynamic_slice_in_dim(queries, xlo * SPAN, SPAN, 0)
    q_got = flip(after(give, packed), "xlo")
    kv_own = jnp.stack([packed, kv_xlo, kv_core, kv_both])
    meta = jnp.stack([xlo, z, core])
    attend = functools.partial(attention, meta, span_order, cache_length, q_own, q_got)
    ring1 = outward(kv_own)
    cross1 = flip(ring1, "core")
    w_gated = after(out_weight, ring1, q_got)
    w_xlo, w_core = flip(w_gated, "xlo"), flip(w_gated, "core")
    ring2 = outward(ring1)
    cross2 = flip(ring2, "core")
    state = attend([kv_own, ring1], [parts_of(0, 0, 0), parts_of(1, 0, 1)], None)
    ring3 = outward(after(ring2, state[0]))
    cross3 = flip(ring3, "core")
    state = attend([ring2, cross1], [parts_of(0, 0, 2), parts_of(1, 1, 1)], state)
    ring4 = outward(after(ring3[:2], state[0], w_core))
    state = attend([ring3, cross2], [parts_of(0, 0, 3), parts_of(1, 1, 2)], state)
    cross4 = flip(after(ring4, state[1]), "core")
    far_slots = [parts_of(0, 1, 3), parts_of(1, 0, 4, 2) + parts_of(2, 1, 4, 2)]
    attended = attend([cross3, ring4, cross4], far_slots, state, True)

    meta_project = jnp.stack([xlo, z, y, xhi])

    def both_ways(up, down, *others):
        return shift(after(up, *others), "z", 1), shift(after(down, *others), "z", -1)

    def place_near(own, up, down):
        return place_rows(meta_project, [own, up, down], (0, -1, 1))

    def place_far(rows, up, down):
        return place_rows(meta_project, [up, down], (-2, 2), rows)

    distances = ((-3, (0, 1)), (3, (0, 1)), (4, (0,)), (4, (1,)))
    first, second = attended
    a1 = both_ways(first, first)
    a2 = both_ways(*a1)
    near_a = place_near(first, *a1)
    b1 = both_ways(second, second, near_a)
    a3 = both_ways(*a2, near_a)
    held_a = place_far(near_a, *a2)
    b2 = both_ways(*b1, held_a)
    near_b = place_near(second, *b1)
    a4 = both_ways(a3[0][:1], a3[1][1:], near_b)
    w_both = flip(after(w_xlo, *a3, *b2), "core")
    weights = [out_weight, w_core, w_xlo, w_both]
    b3 = both_ways(*b2, near_b, *a3)
    held_b = place_far(near_b, *b2)
    b4 = both_ways(b3[0][:1], b3[1][1:], held_b, *a4)
    sends_a = project(meta_project, after(held_a, *b3, held_b), [*a3, *a4], distances, weights, 0)
    sends_b = project(meta_project, after(held_b, sends_a[0]), [*b3, *b4], distances, weights, 0)
    rest_a = project(meta_project, held_a, [*a3, *a4], distances, weights, 1)
    rest_b = project(meta_project, held_b, [*b3, *b4], distances, weights, 1)

    pieces = []
    for (plus, minus), (own_a, own_b, p1a, p3b) in ((sends_a, rest_a), (sends_b, rest_b)):
        plus, minus = shift(plus, "y", 1), shift(minus, "y", -1)
        sum_a, sum_b = add2(p1a, plus[: 2 * ROWS]), add2(p3b, minus[: 2 * ROWS])
        in1a, in3b = shift(sum_a, "y", 1), shift(sum_b, "y", -1)
        give_b = (own_b.astype(F32) + plus[2 * ROWS :].astype(F32) + in3b.astype(F32)).astype(BF16)
        got_a = flip(give_b, "xhi")
        mine, to_core, to_xlo, to_both = last_sum(own_a, in1a, minus, got_a)
        pieces += [mine, flip(to_core, "core"), flip(to_xlo, "xlo"), flip_both(to_both)]
    mixed = assemble(jnp.stack([xlo, core]), pieces)
    paged_keys = seg_keys.reshape(seg_keys.shape[0] // PAGE, PAGE, seg_keys.shape[1])
    return (mixed, jnp.min(paged_keys, axis=1), jnp.max(paged_keys, axis=1))


def solution(mesh):
    split = Mesh(mesh.devices.reshape(2, NZ, 2, 4, 2), ("xlo", "z", "core", "y", "xhi"))
    ctx, head = ("xlo", "z", "core"), ("y", "xhi")
    in_specs = (
        P(ctx, head),
        P(ctx, head),
        P(ctx, head),
        P(ctx, head),
        P(ctx, head),
        P(),
        P(),
        P(head, ctx),
    )
    out_specs = (P(head, ctx), P(ctx, head), P(ctx, head))
    return jax.shard_map(shards, mesh=split, in_specs=in_specs, out_specs=out_specs, check_vma=False)
```

```python
import functools
import math

import jax
import jax.numpy as jnp
from jax import lax
from jax.experimental import pallas as pl
from jax.experimental.pallas import tpu as pltpu
from jax.sharding import Mesh
from jax.sharding import PartitionSpec as P

HD = 128
GROUP = 16
PAGE = 16
SPAN = 64
NZ = 8
CHUNKS = 2
ROWS = SPAN // CHUNKS
WIDTH = GROUP * HD
LOG2E = 1.4426950408889634
HIDDEN = -1e30
KEYS = 640
HALVES = 2
F32 = jnp.float32
BF16 = jnp.bfloat16


def shift(block, axis, distance):
    n = lax.axis_size(axis)
    return lax.ppermute(block, axis, [(i, (i + distance) % n) for i in range(n)])


def flip(block, axis):
    return shift(block, axis, 1)


def flip_both(block):
    return lax.ppermute(block, ("xlo", "core"), [(i, 3 - i) for i in range(4)])


def outward(block):
    route = []
    for z in range(NZ):
        route.append((2 * z, 2 * ((z + 1) % NZ)))
        route.append((2 * z + 1, 2 * ((z - 1) % NZ) + 1))
    return lax.ppermute(block, ("z", "core"), route)


def pack_kernel(k, v, ck, cv, out):
    out[0:128] = k[...].T
    out[128:256] = v[...]
    out[256:288] = ck[...]
    out[288:320] = cv[...]


def pack(k, v, ck, cv):
    return pl.pallas_call(
        pack_kernel,
        out_shape=jax.ShapeDtypeStruct((320, HD), BF16),
        name="pack",
    )(k, v, ck, cv)


def attention_kernel(meta, order, length, q_own, q_got, *rest, slots, scale, first, last):
    n_refs = 1 + max(part[0] for slot in slots for part in slot)
    kv_refs, rest = rest[:n_refs], rest[n_refs:]
    if not first:
        top_in, acc_in, rest = rest[0], rest[1], rest[2:]
    tile = pl.program_id(0)
    span = tile % 2
    xlo, z, core = meta[0], meta[1], meta[2]
    first_row = tile // 2 * ROWS
    lane128 = lax.broadcasted_iota(jnp.int32, (1, 128), 1)

    def source_of(side, part, distance):
        sign = jnp.where((core + side) % 2 == 0, -1, 1)
        sz = (z + sign * distance + NZ) % NZ
        return ((xlo + part % 2) % 2) * 16 + sz * 2 + (core + part // 2 + side) % 2

    own_place = order[2 * (xlo * 16 + z * 2 + core) + xlo]
    got_place = order[2 * ((1 - xlo) * 16 + z * 2 + core) + xlo]
    mine = span == xlo
    my_place = jnp.where(mine, own_place, got_place)
    q_rows = jnp.where(mine, q_own[...], q_got[...])
    half_heads = GROUP // HALVES
    half_rows = half_heads * ROWS
    q_tiles = [
        jnp.concatenate([q_rows[:, i * HD : (i + 1) * HD] for i in range(h * half_heads, (h + 1) * half_heads)], axis=0)
        for h in range(HALVES)
    ]

    keys, values, biases, diagonal = [], [], [], None
    for slot in slots:
        parts = [kv_refs[ref].at[place] for ref, place, *_ in slot]
        block = jnp.concatenate(
            [p[0:128] for p in parts] + [jnp.concatenate([p[256:288] for p in parts], axis=0).T], axis=1
        )
        block_values = jnp.concatenate([p[128:256] for p in parts] + [p[288:320] for p in parts], axis=0)
        values.append(jnp.concatenate([block_values, jnp.ones((KEYS, HD), BF16)], axis=1))
        places = []
        cache_slot = lane128 % 32
        for i, (_, _, side, part, distance) in enumerate(slot):
            ctx = source_of(side, part, distance)
            places.append(jnp.where(lane128 < SPAN, order[2 * ctx], order[2 * ctx + 1]))
            cache_slot = jnp.where(lane128 // 32 == i, cache_slot + ctx * 32, cache_slot)
        places.append(jnp.where(cache_slot < length[0], -1, 64))
        places = jnp.concatenate(places, axis=1)
        has_diagonal = slot[0][4] == 0
        biases.append(jnp.where(places < my_place, 0.0, HIDDEN))
        if has_diagonal:
            lane = lax.broadcasted_iota(jnp.int32, (1, KEYS), 1) % SPAN
            diagonal = jnp.where(places == my_place, lane, 1000)
        keys.append(block)
    row = lax.broadcasted_iota(jnp.int32, (half_rows, 1), 0) % ROWS + first_row

    def scores_of(h, i):
        s = jnp.dot(q_tiles[h], keys[i], preferred_element_type=F32) * scale
        if slots[i][0][4] == 0:
            return jnp.where(diagonal <= row, s, s + biases[i])
        return s + biases[i]

    tops, accs = [], []
    for h in range(HALVES):
        at = slice(h * half_rows, (h + 1) * half_rows)
        scores = [scores_of(h, i) for i in range(len(slots))]
        pieces = [s[:, i * 128 : (i + 1) * 128] for s in scores for i in range(5)]
        peak = functools.reduce(jnp.maximum, pieces)
        top = jnp.broadcast_to(jnp.max(peak, axis=1, keepdims=True), (half_rows, 128))
        if not first:
            top = jnp.maximum(top_in[at], top)
            factor = jnp.exp2(top_in[at] - top)
            acc = acc_in[at] * jnp.concatenate([factor, factor], axis=1)
        else:
            acc = None
        for i in range(len(slots)):
            weights = jnp.concatenate(
                [jnp.exp2(p - top) for p in pieces[5 * i : 5 * i + 5]], axis=1
            ).astype(BF16)
            added = jnp.dot(weights, values[i], preferred_element_type=F32)
            acc = added if acc is None else acc + added
        tops.append(top)
        accs.append(acc)

    if last:
        for chunk in range(CHUNKS):

            @pl.when(tile // 2 == chunk)
            def _():
                for h in range(HALVES):
                    result = (accs[h][:, :HD] / accs[h][:, HD:]).astype(BF16)
                    for i in range(half_heads):
                        col = (h * half_heads + i) * HD
                        rest[chunk][0, :, col : col + HD] = result[i * ROWS : (i + 1) * ROWS]
    else:
        top_out, acc_out = rest
        for h in range(HALVES):
            top_out[h * half_rows : (h + 1) * half_rows] = tops[h]
            acc_out[h * half_rows : (h + 1) * half_rows] = accs[h]


def attention(meta, order, length, q_own, q_got, kv_blocks, slots, state, last=False):
    first = state is None
    tile_rows = ROWS * GROUP
    tiles = 2 * CHUNKS
    q_spec = pl.BlockSpec((ROWS, WIDTH), lambda step, *_: (step // 2, 0))
    whole = [pl.BlockSpec(b.shape, lambda step, *_: (0, 0, 0)) for b in kv_blocks]
    state_specs = [pl.BlockSpec((tile_rows, w), lambda step, *_: (step, 0)) for w in (HD, 2 * HD)]
    if last:

        def chunk_spec(chunk):
            return pl.BlockSpec((1, ROWS, WIDTH), lambda step, *_: (jnp.clip(step - 2 * chunk, 0, 1), 0, 0))

        out_shape = [jax.ShapeDtypeStruct((2, ROWS, WIDTH), BF16)] * CHUNKS
        out_specs = [chunk_spec(chunk) for chunk in range(CHUNKS)]
    else:
        out_shape = [jax.ShapeDtypeStruct((tiles * tile_rows, w), F32) for w in (HD, 2 * HD)]
        out_specs = state_specs
    work = tiles * tile_rows * KEYS * len(slots)
    return pl.pallas_call(
        functools.partial(attention_kernel, slots=slots, scale=LOG2E / math.sqrt(HD), first=first, last=last),
        out_shape=out_shape,
        grid_spec=pltpu.PrefetchScalarGridSpec(
            num_scalar_prefetch=3,
            grid=(tiles,),
            in_specs=[q_spec, q_spec] + whole + ([] if first else state_specs),
            out_specs=out_specs,
        ),
        compiler_params=pltpu.CompilerParams(vmem_limit_bytes=20 * 1024 * 1024),
        cost_estimate=pl.CostEstimate(flops=work * 32, bytes_accessed=2**18, transcendentals=work // 64),
        name="attention",
    )(meta, order, length, q_own, q_got, *kv_blocks, *([] if first else state))


def parts_of(ref, side, distance, count=4, offset=0):
    return [(ref, i, side, offset + i, distance) for i in range(count)]


def slot_of(meta, s, distance):
    z, y, xhi = meta[1], meta[2], meta[3]
    place = (z + distance + NZ) % NZ
    part = (2 * s + place // 4 - y + 4) % 4
    other = (place // 2 + xhi) % 2
    index = 2 * part + other
    group = jnp.int32(7)
    for position, key in enumerate((4, 3, 5, 6, 0, 1, 2)):
        group = jnp.where(index == key, position, group)
    return 2 * group + place % 2


def place_kernel(meta, *refs, distances):
    n = len(distances)
    sources, out, sem = refs[:n], refs[-2], refs[-1]
    copies = []
    for source, distance in zip(sources, distances):
        for s in range(2):
            row = slot_of(meta, s, distance) * ROWS
            copies.append(
                pltpu.make_async_copy(
                    source.at[s], out.at[pl.ds(pl.multiple_of(row, ROWS), ROWS)], sem.at[len(copies)]
                )
            )
    for c in copies:
        c.start()
    for c in copies:
        c.wait()


def place_rows(meta, sources, distances, rows=None):
    fresh = rows is None
    n = len(sources)
    return pl.pallas_call(
        functools.partial(place_kernel, distances=distances),
        out_shape=jax.ShapeDtypeStruct((16 * ROWS, WIDTH), BF16),
        in_specs=[SMEM_SPEC] + [VMEM_SPEC] * n + ([] if fresh else [pl.BlockSpec(memory_space=pl.ANY)]),
        out_specs=pl.BlockSpec(memory_space=pl.ANY),
        scratch_shapes=[pltpu.SemaphoreType.DMA((2 * n,))],
        input_output_aliases={} if fresh else {n + 1: 0},
        compiler_params=pltpu.CompilerParams(vmem_limit_bytes=4 * 1024 * 1024),
        name="place_rows",
    )(meta, *sources, *([] if fresh else [rows]))


SMEM_SPEC = pl.BlockSpec(memory_space=pltpu.SMEM)
VMEM_SPEC = pl.BlockSpec(memory_space=pltpu.VMEM)


def project_kernel(meta, held, *refs, late, group):
    n = len(late)
    sources, w_refs, outs, rows, sem = refs[:n], refs[n : n + 4], refs[n + 4 : -2], refs[-2], refs[-1]
    mine = pl.ds(group * 8 * ROWS, 8 * ROWS)
    copy = pltpu.make_async_copy(held.at[mine], rows.at[mine], sem)
    copy.start()
    copy.wait()
    for source, (distance, halves) in zip(sources, late):
        for i, s in enumerate(halves):
            row = slot_of(meta, s, distance) * ROWS
            rows[pl.ds(pl.multiple_of(row, ROWS), ROWS)] = source[i]
    for i in range(4):
        total = jnp.dot(rows[mine], w_refs[i][...], preferred_element_type=F32).astype(BF16)
        size = 8 * ROWS // len(outs)
        for k, out in enumerate(outs):
            out[:, 512 * i : 512 * (i + 1)] = total[k * size : (k + 1) * size]


def project(meta, held, late, distances, weights, group):
    count = (2, 4)[group]
    return pl.pallas_call(
        functools.partial(project_kernel, late=distances, group=group),
        out_shape=[jax.ShapeDtypeStruct((8 * ROWS // count, 2048), BF16)] * count,
        in_specs=[SMEM_SPEC, pl.BlockSpec(memory_space=pl.ANY)] + [VMEM_SPEC] * (len(late) + 4),
        out_specs=[VMEM_SPEC] * count,
        scratch_shapes=[pltpu.VMEM((16 * ROWS, WIDTH), BF16), pltpu.SemaphoreType.DMA],
        compiler_params=pltpu.CompilerParams(vmem_limit_bytes=12 * 1024 * 1024),
        cost_estimate=pl.CostEstimate(flops=16 * ROWS * 2048 * 2048, bytes_accessed=1 * 2**20, transcendentals=0),
        name="project",
    )(meta, held, *late, *weights)


def add2(x, y):
    return (x.astype(F32) + y.astype(F32)).astype(BF16)


def last_sum_kernel(x, y, z, u, *outs):
    total = x[...].astype(F32) + y[...].astype(F32) + z[2 * ROWS :].astype(F32) + u[...].astype(F32)
    for i, out in enumerate(outs):
        out[...] = total[:, 512 * i : 512 * (i + 1)].astype(BF16)


def last_sum(*terms):
    return pl.pallas_call(
        last_sum_kernel,
        out_shape=[jax.ShapeDtypeStruct((2 * ROWS, 512), BF16)] * 4,
        in_specs=[VMEM_SPEC] * 4,
        out_specs=[VMEM_SPEC] * 4,
        compiler_params=pltpu.CompilerParams(vmem_limit_bytes=4 * 1024 * 1024),
        name="last_sum",
    )(*terms)


def assemble_kernel(meta, *refs):
    pieces, out = refs[:-1], refs[-1]
    xlo, core = meta[0], meta[1]
    for j in range(CHUNKS):
        for i in range(4):
            from_core = (core + i % 2) % 2
            from_xlo = (xlo + i // 2) % 2
            for zi in range(2):
                row = (zi * 2 + from_core) * 128 + from_xlo * SPAN + j * ROWS
                out[pl.ds(pl.multiple_of(row, 32), ROWS)] = pieces[4 * j + i][zi * ROWS : (zi + 1) * ROWS]


def assemble(meta, pieces):
    return pl.pallas_call(
        assemble_kernel,
        out_shape=jax.ShapeDtypeStruct((512, 512), BF16),
        in_specs=[SMEM_SPEC] + [VMEM_SPEC] * (4 * CHUNKS),
        out_specs=VMEM_SPEC,
        compiler_params=pltpu.CompilerParams(vmem_limit_bytes=4 * 1024 * 1024),
        name="assemble",
    )(meta, *pieces)


def after(value, *others):
    return lax.optimization_barrier((value, *others))[0]


def shards(
    queries, seg_keys, seg_values, cache_keys, cache_values, span_order, cache_length, out_weight
):
    xlo, z, core = lax.axis_index("xlo"), lax.axis_index("z"), lax.axis_index("core")
    y, xhi = lax.axis_index("y"), lax.axis_index("xhi")

    packed = pack(seg_keys, seg_values, cache_keys, cache_values)
    kv_core, kv_xlo, kv_both = flip(packed, "core"), flip(packed, "xlo"), flip_both(packed)
    give = lax.dynamic_slice_in_dim(queries, (1 - xlo) * SPAN, SPAN, 0)
    q_own = lax.dynamic_slice_in_dim(queries, xlo * SPAN, SPAN, 0)
    q_got = flip(after(give, packed), "xlo")
    kv_own = jnp.stack([packed, kv_xlo, kv_core, kv_both])
    meta = jnp.stack([xlo, z, core])
    attend = functools.partial(attention, meta, span_order, cache_length, q_own, q_got)
    ring1 = outward(kv_own)
    cross1 = flip(ring1, "core")
    w_gated = after(out_weight, ring1, q_got)
    w_xlo, w_core = flip(w_gated, "xlo"), flip(w_gated, "core")
    ring2 = outward(ring1)
    cross2 = flip(ring2, "core")
    state = attend([kv_own, ring1], [parts_of(0, 0, 0), parts_of(1, 0, 1)], None)
    ring3 = outward(after(ring2, state[0]))
    cross3 = flip(ring3, "core")
    state = attend([ring2, cross1], [parts_of(0, 0, 2), parts_of(1, 1, 1)], state)
    ring4 = outward(after(ring3[:2], state[0], w_core))
    state = attend([ring3, cross2], [parts_of(0, 0, 3), parts_of(1, 1, 2)], state)
    cross4 = flip(after(ring4, state[1]), "core")
    far_slots = [parts_of(0, 1, 3), parts_of(1, 0, 4, 2) + parts_of(2, 1, 4, 2)]
    attended = attend([cross3, ring4, cross4], far_slots, state, True)

    meta_project = jnp.stack([xlo, z, y, xhi])

    def both_ways(up, down, *others):
        return shift(after(up, *others), "z", 1), shift(after(down, *others), "z", -1)

    def both_along_y(plus, minus):
        return shift(plus, "y", 1), shift(minus, "y", -1)

    def place_near(own, up, down):
        return place_rows(meta_project, [own, up, down], (0, -1, 1))

    def place_far(rows, up, down):
        return place_rows(meta_project, [up, down], (-2, 2), rows)

    distances = ((-3, (0, 1)), (3, (0, 1)), (4, (0,)), (4, (1,)))
    first, second = attended
    a1 = both_ways(first, first)
    b1 = both_ways(second, second)
    a2 = both_ways(*a1)
    near_a = place_near(first, *a1)
    b2 = both_ways(*b1, near_a)
    a3 = both_ways(*a2, near_a)
    near_b = place_near(second, *b1)
    held_a = place_far(near_a, *a2)
    w_both = flip(after(w_xlo, *a3, *b2), "core")
    weights = [out_weight, w_core, w_xlo, w_both]
    b3 = both_ways(*b2, near_b)
    a4 = both_ways(a3[0][:1], a3[1][1:], held_a)
    held_b = place_far(near_b, *b2)
    b4 = both_ways(b3[0][:1], b3[1][1:], held_b)
    late_a, late_b = [*a3, *a4], [*b3, *b4]
    project_rows = functools.partial(project, meta_project)

    plus_a, minus_a = project_rows(after(held_a, *b3, held_b), late_a, distances, weights, 0)
    plus_b, minus_b = project_rows(after(held_b, plus_a), late_b, distances, weights, 0)
    sums_a, sums_b = both_along_y(plus_a, minus_a), both_along_y(plus_b, minus_b)
    rest_a = project_rows(held_a, late_a, distances, weights, 1)
    rest_b = project_rows(after(held_b, *sums_a), late_b, distances, weights, 1)

    pieces = []
    for (plus, minus), (own_a, own_b, p1a, p3b) in ((sums_a, rest_a), (sums_b, rest_b)):
        in1a, in3b = both_along_y(add2(p1a, plus[: 2 * ROWS]), add2(p3b, minus[: 2 * ROWS]))
        give_b = (own_b.astype(F32) + plus[2 * ROWS :].astype(F32) + in3b.astype(F32)).astype(BF16)
        got_a = flip(give_b, "xhi")
        mine, to_core, to_xlo, to_both = last_sum(own_a, in1a, minus, got_a)
        pieces += [mine, flip(to_core, "core"), flip(to_xlo, "xlo"), flip_both(to_both)]
    mixed = assemble(jnp.stack([xlo, core]), pieces)
    paged_keys = seg_keys.reshape(seg_keys.shape[0] // PAGE, PAGE, seg_keys.shape[1])
    return (mixed, jnp.min(paged_keys, axis=1), jnp.max(paged_keys, axis=1))


def solution(mesh):
    split = Mesh(mesh.devices.reshape(2, NZ, 2, 4, 2), ("xlo", "z", "core", "y", "xhi"))
    ctx, head = ("xlo", "z", "core"), ("y", "xhi")
    in_specs = (
        P(ctx, head),
        P(ctx, head),
        P(ctx, head),
        P(ctx, head),
        P(ctx, head),
        P(),
        P(),
        P(head, ctx),
    )
    out_specs = (P(head, ctx), P(ctx, head), P(ctx, head))
    return jax.shard_map(shards, mesh=split, in_specs=in_specs, out_specs=out_specs, check_vma=False)
```

```python
import functools
import math

import jax
import jax.numpy as jnp
from jax import lax
from jax.experimental import pallas as pl
from jax.experimental.pallas import tpu as pltpu
from jax.sharding import Mesh
from jax.sharding import PartitionSpec as P

HD = 128
GROUP = 16
PAGE = 16
SPAN = 64
NZ = 8
CHUNKS = 2
ROWS = SPAN // CHUNKS
WIDTH = GROUP * HD
LOG2E = 1.4426950408889634
HIDDEN = -1e30
KEYS = 640
HALVES = 2
F32 = jnp.float32
BF16 = jnp.bfloat16


def shift(block, axis, distance):
    n = lax.axis_size(axis)
    return lax.ppermute(block, axis, [(i, (i + distance) % n) for i in range(n)])


def flip(block, axis):
    return shift(block, axis, 1)


def flip_both(block):
    return lax.ppermute(block, ("xlo", "core"), [(i, 3 - i) for i in range(4)])


def outward(block):
    route = []
    for z in range(NZ):
        route.append((2 * z, 2 * ((z + 1) % NZ)))
        route.append((2 * z + 1, 2 * ((z - 1) % NZ) + 1))
    return lax.ppermute(block, ("z", "core"), route)


def pack_kernel(k, v, ck, cv, out):
    out[0:128] = k[...].T
    out[128:256] = v[...]
    out[256:288] = ck[...]
    out[288:320] = cv[...]


def pack(k, v, ck, cv):
    return pl.pallas_call(
        pack_kernel,
        out_shape=jax.ShapeDtypeStruct((320, HD), BF16),
        name="pack",
    )(k, v, ck, cv)


def attention_kernel(meta, order, length, q_own, q_got, *rest, slots, scale, first, last):
    n_refs = 1 + max(part[0] for slot in slots for part in slot)
    kv_refs, rest = rest[:n_refs], rest[n_refs:]
    if not first:
        top_in, acc_in, rest = rest[0], rest[1], rest[2:]
    tile = pl.program_id(0)
    span = tile % 2
    xlo, z, core = meta[0], meta[1], meta[2]
    first_row = tile // 2 * ROWS
    lane128 = lax.broadcasted_iota(jnp.int32, (1, 128), 1)

    def source_of(side, part, distance):
        sign = jnp.where((core + side) % 2 == 0, -1, 1)
        sz = (z + sign * distance + NZ) % NZ
        return ((xlo + part % 2) % 2) * 16 + sz * 2 + (core + part // 2 + side) % 2

    own_place = order[2 * (xlo * 16 + z * 2 + core) + xlo]
    got_place = order[2 * ((1 - xlo) * 16 + z * 2 + core) + xlo]
    mine = span == xlo
    my_place = jnp.where(mine, own_place, got_place)
    q_rows = jnp.where(mine, q_own[...], q_got[...])
    half_heads = GROUP // HALVES
    half_rows = half_heads * ROWS
    q_tiles = [
        jnp.concatenate([q_rows[:, i * HD : (i + 1) * HD] for i in range(h * half_heads, (h + 1) * half_heads)], axis=0)
        for h in range(HALVES)
    ]

    keys, values, biases, diagonal = [], [], [], None
    for slot in slots:
        parts = [kv_refs[ref].at[place] for ref, place, *_ in slot]
        block = jnp.concatenate(
            [p[0:128] for p in parts] + [jnp.concatenate([p[256:288] for p in parts], axis=0).T], axis=1
        )
        block_values = jnp.concatenate([p[128:256] for p in parts] + [p[288:320] for p in parts], axis=0)
        values.append(jnp.concatenate([block_values, jnp.ones((KEYS, HD), BF16)], axis=1))
        places = []
        cache_slot = lane128 % 32
        for i, (_, _, side, part, distance) in enumerate(slot):
            ctx = source_of(side, part, distance)
            places.append(jnp.where(lane128 < SPAN, order[2 * ctx], order[2 * ctx + 1]))
            cache_slot = jnp.where(lane128 // 32 == i, cache_slot + ctx * 32, cache_slot)
        places.append(jnp.where(cache_slot < length[0], -1, 64))
        places = jnp.concatenate(places, axis=1)
        has_diagonal = slot[0][4] == 0
        biases.append(jnp.where(places < my_place, 0.0, HIDDEN))
        if has_diagonal:
            lane = lax.broadcasted_iota(jnp.int32, (1, KEYS), 1) % SPAN
            diagonal = jnp.where(places == my_place, lane, 1000)
        keys.append(block)
    row = lax.broadcasted_iota(jnp.int32, (half_rows, 1), 0) % ROWS + first_row

    def scores_of(h, i):
        s = jnp.dot(q_tiles[h], keys[i], preferred_element_type=F32) * scale
        if slots[i][0][4] == 0:
            return jnp.where(diagonal <= row, s, s + biases[i])
        return s + biases[i]

    tops, accs = [], []
    for h in range(HALVES):
        at = slice(h * half_rows, (h + 1) * half_rows)
        scores = [scores_of(h, i) for i in range(len(slots))]
        pieces = [s[:, i * 128 : (i + 1) * 128] for s in scores for i in range(5)]
        peak = functools.reduce(jnp.maximum, pieces)
        top = jnp.broadcast_to(jnp.max(peak, axis=1, keepdims=True), (half_rows, 128))
        if not first:
            top = jnp.maximum(top_in[at], top)
            factor = jnp.exp2(top_in[at] - top)
            acc = acc_in[at] * jnp.concatenate([factor, factor], axis=1)
        else:
            acc = None
        for i in range(len(slots)):
            weights = jnp.concatenate(
                [jnp.exp2(p - top) for p in pieces[5 * i : 5 * i + 5]], axis=1
            ).astype(BF16)
            added = jnp.dot(weights, values[i], preferred_element_type=F32)
            acc = added if acc is None else acc + added
        tops.append(top)
        accs.append(acc)

    if last:
        for chunk in range(CHUNKS):

            @pl.when(tile // 2 == chunk)
            def _():
                for h in range(HALVES):
                    result = (accs[h][:, :HD] / accs[h][:, HD:]).astype(BF16)
                    for i in range(half_heads):
                        col = (h * half_heads + i) * HD
                        rest[chunk][0, :, col : col + HD] = result[i * ROWS : (i + 1) * ROWS]
    else:
        top_out, acc_out = rest
        for h in range(HALVES):
            top_out[h * half_rows : (h + 1) * half_rows] = tops[h]
            acc_out[h * half_rows : (h + 1) * half_rows] = accs[h]


def attention(meta, order, length, q_own, q_got, kv_blocks, slots, state, last=False):
    first = state is None
    tile_rows = ROWS * GROUP
    tiles = 2 * CHUNKS
    q_spec = pl.BlockSpec((ROWS, WIDTH), lambda step, *_: (step // 2, 0))
    whole = [pl.BlockSpec(b.shape, lambda step, *_: (0, 0, 0)) for b in kv_blocks]
    state_specs = [pl.BlockSpec((tile_rows, w), lambda step, *_: (step, 0)) for w in (HD, 2 * HD)]
    if last:

        def chunk_spec(chunk):
            return pl.BlockSpec((1, ROWS, WIDTH), lambda step, *_: (jnp.clip(step - 2 * chunk, 0, 1), 0, 0))

        out_shape = [jax.ShapeDtypeStruct((2, ROWS, WIDTH), BF16)] * CHUNKS
        out_specs = [chunk_spec(chunk) for chunk in range(CHUNKS)]
    else:
        out_shape = [jax.ShapeDtypeStruct((tiles * tile_rows, w), F32) for w in (HD, 2 * HD)]
        out_specs = state_specs
    work = tiles * tile_rows * KEYS * len(slots)
    return pl.pallas_call(
        functools.partial(attention_kernel, slots=slots, scale=LOG2E / math.sqrt(HD), first=first, last=last),
        out_shape=out_shape,
        grid_spec=pltpu.PrefetchScalarGridSpec(
            num_scalar_prefetch=3,
            grid=(tiles,),
            in_specs=[q_spec, q_spec] + whole + ([] if first else state_specs),
            out_specs=out_specs,
        ),
        compiler_params=pltpu.CompilerParams(vmem_limit_bytes=20 * 1024 * 1024),
        cost_estimate=pl.CostEstimate(flops=work * 32, bytes_accessed=2**18, transcendentals=work // 64),
        name="attention",
    )(meta, order, length, q_own, q_got, *kv_blocks, *([] if first else state))


def parts_of(ref, side, distance, count=4, offset=0):
    return [(ref, i, side, offset + i, distance) for i in range(count)]


def slot_of(meta, s, distance):
    z, y, xhi = meta[1], meta[2], meta[3]
    place = (z + distance + NZ) % NZ
    part = (2 * s + place // 4 - y + 4) % 4
    other = (place // 2 + xhi) % 2
    index = 2 * part + other
    group = jnp.int32(7)
    for position, key in enumerate((4, 3, 5, 6, 0, 1, 2)):
        group = jnp.where(index == key, position, group)
    return 2 * group + place % 2


def place_kernel(meta, *refs, distances):
    n = len(distances)
    sources, out, sem = refs[:n], refs[-2], refs[-1]
    copies = []
    for source, distance in zip(sources, distances):
        for s in range(2):
            row = slot_of(meta, s, distance) * ROWS
            copies.append(
                pltpu.make_async_copy(
                    source.at[s], out.at[pl.ds(pl.multiple_of(row, ROWS), ROWS)], sem.at[len(copies)]
                )
            )
    for c in copies:
        c.start()
    for c in copies:
        c.wait()


def place_rows(meta, sources, distances, rows=None):
    fresh = rows is None
    n = len(sources)
    return pl.pallas_call(
        functools.partial(place_kernel, distances=distances),
        out_shape=jax.ShapeDtypeStruct((16 * ROWS, WIDTH), BF16),
        in_specs=[SMEM_SPEC] + [VMEM_SPEC] * n + ([] if fresh else [pl.BlockSpec(memory_space=pl.ANY)]),
        out_specs=pl.BlockSpec(memory_space=pl.ANY),
        scratch_shapes=[pltpu.SemaphoreType.DMA((2 * n,))],
        input_output_aliases={} if fresh else {n + 1: 0},
        compiler_params=pltpu.CompilerParams(vmem_limit_bytes=4 * 1024 * 1024),
        name="place_rows",
    )(meta, *sources, *([] if fresh else [rows]))


SMEM_SPEC = pl.BlockSpec(memory_space=pltpu.SMEM)
VMEM_SPEC = pl.BlockSpec(memory_space=pltpu.VMEM)


def project_kernel(meta, held, *refs, late, group):
    n = len(late)
    sources, w_refs, outs, rows, sem = refs[:n], refs[n : n + 4], refs[n + 4 : -2], refs[-2], refs[-1]
    mine = pl.ds(group * 8 * ROWS, 8 * ROWS)
    copy = pltpu.make_async_copy(held.at[mine], rows.at[mine], sem)
    copy.start()
    copy.wait()
    for source, (distance, halves) in zip(sources, late):
        for i, s in enumerate(halves):
            row = slot_of(meta, s, distance) * ROWS
            rows[pl.ds(pl.multiple_of(row, ROWS), ROWS)] = source[i]
    for i in range(4):
        total = jnp.dot(rows[mine], w_refs[i][...], preferred_element_type=F32).astype(BF16)
        size = 8 * ROWS // len(outs)
        for k, out in enumerate(outs):
            out[:, 512 * i : 512 * (i + 1)] = total[k * size : (k + 1) * size]


def project(meta, held, late, distances, weights, group):
    count = (2, 4)[group]
    return pl.pallas_call(
        functools.partial(project_kernel, late=distances, group=group),
        out_shape=[jax.ShapeDtypeStruct((8 * ROWS // count, 2048), BF16)] * count,
        in_specs=[SMEM_SPEC, pl.BlockSpec(memory_space=pl.ANY)] + [VMEM_SPEC] * (len(late) + 4),
        out_specs=[VMEM_SPEC] * count,
        scratch_shapes=[pltpu.VMEM((16 * ROWS, WIDTH), BF16), pltpu.SemaphoreType.DMA],
        compiler_params=pltpu.CompilerParams(vmem_limit_bytes=12 * 1024 * 1024),
        cost_estimate=pl.CostEstimate(flops=16 * ROWS * 2048 * 2048, bytes_accessed=1 * 2**20, transcendentals=0),
        name="project",
    )(meta, held, *late, *weights)


def add2(x, y):
    return (x.astype(F32) + y.astype(F32)).astype(BF16)


def last_sum_kernel(*refs):
    terms, outs = refs[:-4], refs[-4:]
    rows = 2 * ROWS
    for j in range(CHUNKS):
        x, y, z, u = terms[4 * j : 4 * j + 4]
        total = x[...].astype(F32) + y[...].astype(F32) + z[rows:].astype(F32) + u[...].astype(F32)
        for i, out in enumerate(outs):
            out[j * rows : (j + 1) * rows] = total[:, 512 * i : 512 * (i + 1)].astype(BF16)


def last_sum(*terms):
    return pl.pallas_call(
        last_sum_kernel,
        out_shape=[jax.ShapeDtypeStruct((2 * ROWS * CHUNKS, 512), BF16)] * 4,
        in_specs=[VMEM_SPEC] * (4 * CHUNKS),
        out_specs=[VMEM_SPEC] * 4,
        compiler_params=pltpu.CompilerParams(vmem_limit_bytes=4 * 1024 * 1024),
        name="last_sum",
    )(*terms)


def assemble_kernel(meta, *refs):
    pieces, out = refs[:-1], refs[-1]
    xlo, core = meta[0], meta[1]
    for j in range(CHUNKS):
        for i in range(4):
            from_core = (core + i % 2) % 2
            from_xlo = (xlo + i // 2) % 2
            for zi in range(2):
                row = (zi * 2 + from_core) * 128 + from_xlo * SPAN + j * ROWS
                out[pl.ds(pl.multiple_of(row, 32), ROWS)] = pieces[i][(2 * j + zi) * ROWS : (2 * j + zi + 1) * ROWS]


def assemble(meta, pieces):
    return pl.pallas_call(
        assemble_kernel,
        out_shape=jax.ShapeDtypeStruct((512, 512), BF16),
        in_specs=[SMEM_SPEC] + [VMEM_SPEC] * 4,
        out_specs=VMEM_SPEC,
        compiler_params=pltpu.CompilerParams(vmem_limit_bytes=4 * 1024 * 1024),
        name="assemble",
    )(meta, *pieces)


def after(value, *others):
    return lax.optimization_barrier((value, *others))[0]


def shards(
    queries, seg_keys, seg_values, cache_keys, cache_values, span_order, cache_length, out_weight
):
    xlo, z, core = lax.axis_index("xlo"), lax.axis_index("z"), lax.axis_index("core")
    y, xhi = lax.axis_index("y"), lax.axis_index("xhi")

    packed = pack(seg_keys, seg_values, cache_keys, cache_values)
    kv_core, kv_xlo, kv_both = flip(packed, "core"), flip(packed, "xlo"), flip_both(packed)
    give = lax.dynamic_slice_in_dim(queries, (1 - xlo) * SPAN, SPAN, 0)
    q_own = lax.dynamic_slice_in_dim(queries, xlo * SPAN, SPAN, 0)
    q_got = flip(after(give, packed), "xlo")
    kv_own = jnp.stack([packed, kv_xlo, kv_core, kv_both])
    paged_keys = seg_keys.reshape(seg_keys.shape[0] // PAGE, PAGE, seg_keys.shape[1])
    page_min, page_max = jnp.min(paged_keys, axis=1), jnp.max(paged_keys, axis=1)
    meta = jnp.stack([xlo, z, core])
    attend = functools.partial(attention, meta, span_order, cache_length, q_own, q_got)
    ring1 = outward(kv_own)
    cross1 = flip(ring1, "core")
    w_gated = after(out_weight, ring1, q_got)
    w_xlo, w_core = flip(w_gated, "xlo"), flip(w_gated, "core")
    ring2 = outward(ring1)
    cross2 = flip(ring2, "core")
    state = attend([kv_own, ring1], [parts_of(0, 0, 0), parts_of(1, 0, 1)], None)
    ring3 = outward(after(ring2, state[0]))
    cross3 = flip(ring3, "core")
    state = attend([ring2, cross1], [parts_of(0, 0, 2), parts_of(1, 1, 1)], state)
    ring4 = outward(after(ring3[:2], state[0], w_core))
    state = attend([ring3, cross2], [parts_of(0, 0, 3), parts_of(1, 1, 2)], state)
    cross4 = flip(after(ring4, state[1]), "core")
    far_slots = [parts_of(0, 1, 3), parts_of(1, 0, 4, 2) + parts_of(2, 1, 4, 2)]
    attended = attend([cross3, ring4, cross4], far_slots, state, True)

    meta_project = after(jnp.stack([xlo, z, y, xhi]), page_min, page_max)

    def both_ways(up, down, *others):
        return shift(after(up, *others), "z", 1), shift(after(down, *others), "z", -1)

    def both_along_y(plus, minus):
        return shift(plus, "y", 1), shift(minus, "y", -1)

    def place_near(own, up, down):
        return place_rows(meta_project, [own, up, down], (0, -1, 1))

    def place_far(rows, up, down):
        return place_rows(meta_project, [up, down], (-2, 2), rows)

    distances = ((-3, (0, 1)), (3, (0, 1)), (4, (0,)), (4, (1,)))
    first, second = attended
    a1 = both_ways(first, first)
    b1 = both_ways(second, second)
    a2 = both_ways(*a1)
    near_a = place_near(first, *a1)
    b2 = both_ways(*b1, near_a)
    held_a = place_far(near_a, *a2)
    a3 = both_ways(*a2, held_a)
    near_b = place_near(second, *b1)
    w_both = flip(after(w_xlo, *a3, *b2), "core")
    weights = [out_weight, w_core, w_xlo, w_both]
    b3 = both_ways(*b2, near_b)
    a4 = both_ways(a3[0][:1], a3[1][1:])
    held_b = place_far(near_b, *b2)
    b4 = both_ways(b3[0][:1], b3[1][1:], held_b)
    late_a, late_b = [*a3, *a4], [*b3, *b4]
    project_rows = functools.partial(project, meta_project)

    plus_a, minus_a = project_rows(after(held_a, *b3, held_b), late_a, distances, weights, 0)
    plus_b, minus_b = project_rows(after(held_b, plus_a), late_b, distances, weights, 0)
    sums_a, sums_b = both_along_y(plus_a, minus_a), both_along_y(plus_b, minus_b)
    rest_a = project_rows(held_a, late_a, distances, weights, 1)
    rest_b = project_rows(after(held_b, *sums_a), late_b, distances, weights, 1)

    terms = []
    for (plus, minus), (own_a, own_b, p1a, p3b) in ((sums_a, rest_a), (sums_b, rest_b)):
        in1a, in3b = both_along_y(add2(p1a, plus[: 2 * ROWS]), add2(p3b, minus[: 2 * ROWS]))
        give_b = (own_b.astype(F32) + plus[2 * ROWS :].astype(F32) + in3b.astype(F32)).astype(BF16)
        terms += [own_a, in1a, minus, flip(give_b, "xhi")]
    mine, to_core, to_xlo, to_both = last_sum(*terms)
    pieces = [mine, flip(to_core, "core"), flip(to_xlo, "xlo"), flip_both(to_both)]
    mixed = assemble(jnp.stack([xlo, core]), pieces)
    return (mixed, page_min, page_max)


def solution(mesh):
    split = Mesh(mesh.devices.reshape(2, NZ, 2, 4, 2), ("xlo", "z", "core", "y", "xhi"))
    ctx, head = ("xlo", "z", "core"), ("y", "xhi")
    in_specs = (
        P(ctx, head),
        P(ctx, head),
        P(ctx, head),
        P(ctx, head),
        P(ctx, head),
        P(),
        P(),
        P(head, ctx),
    )
    out_specs = (P(head, ctx), P(ctx, head), P(ctx, head))
    return jax.shard_map(shards, mesh=split, in_specs=in_specs, out_specs=out_specs, check_vma=False)
```

```python
import functools
import math

import jax
import jax.numpy as jnp
from jax import lax
from jax.experimental import pallas as pl
from jax.experimental.pallas import tpu as pltpu
from jax.sharding import Mesh
from jax.sharding import PartitionSpec as P

HD = 128
GROUP = 16
PAGE = 16
SPAN = 64
NZ = 8
CHUNKS = 2
ROWS = SPAN // CHUNKS
WIDTH = GROUP * HD
LOG2E = 1.4426950408889634
HIDDEN = -1e30
KEYS = 640
HALVES = 2
F32 = jnp.float32
BF16 = jnp.bfloat16


def shift(block, axis, distance):
    n = lax.axis_size(axis)
    return lax.ppermute(block, axis, [(i, (i + distance) % n) for i in range(n)])


def flip(block, axis):
    return shift(block, axis, 1)


def flip_both(block):
    return lax.ppermute(block, ("xlo", "core"), [(i, 3 - i) for i in range(4)])


def outward(block):
    route = []
    for z in range(NZ):
        route.append((2 * z, 2 * ((z + 1) % NZ)))
        route.append((2 * z + 1, 2 * ((z - 1) % NZ) + 1))
    return lax.ppermute(block, ("z", "core"), route)


def pack_kernel(k, v, ck, cv, out):
    out[0:128] = k[...].T
    out[128:256] = v[...]
    out[256:288] = ck[...]
    out[288:320] = cv[...]


def pack(k, v, ck, cv):
    return pl.pallas_call(
        pack_kernel,
        out_shape=jax.ShapeDtypeStruct((320, HD), BF16),
        name="pack",
    )(k, v, ck, cv)


def attention_kernel(meta, order, length, q_own, q_got, *rest, slots, scale, first, last):
    n_refs = 1 + max(part[0] for slot in slots for part in slot)
    kv_refs, rest = rest[:n_refs], rest[n_refs:]
    if not first:
        top_in, acc_in, rest = rest[0], rest[1], rest[2:]
    tile = pl.program_id(0)
    span = tile % 2
    xlo, z, core = meta[0], meta[1], meta[2]
    first_row = tile // 2 * ROWS
    lane128 = lax.broadcasted_iota(jnp.int32, (1, 128), 1)

    def source_of(side, part, distance):
        sign = jnp.where((core + side) % 2 == 0, -1, 1)
        sz = (z + sign * distance + NZ) % NZ
        return ((xlo + part % 2) % 2) * 16 + sz * 2 + (core + part // 2 + side) % 2

    own_place = order[2 * (xlo * 16 + z * 2 + core) + xlo]
    got_place = order[2 * ((1 - xlo) * 16 + z * 2 + core) + xlo]
    mine = span == xlo
    my_place = jnp.where(mine, own_place, got_place)
    q_rows = jnp.where(mine, q_own[...], q_got[...])
    half_heads = GROUP // HALVES
    half_rows = half_heads * ROWS
    q_tiles = [
        jnp.concatenate([q_rows[:, i * HD : (i + 1) * HD] for i in range(h * half_heads, (h + 1) * half_heads)], axis=0)
        for h in range(HALVES)
    ]

    keys, values, biases, diagonal = [], [], [], None
    for slot in slots:
        parts = [kv_refs[ref].at[place] for ref, place, *_ in slot]
        block = jnp.concatenate(
            [p[0:128] for p in parts] + [jnp.concatenate([p[256:288] for p in parts], axis=0).T], axis=1
        )
        block_values = jnp.concatenate([p[128:256] for p in parts] + [p[288:320] for p in parts], axis=0)
        values.append(jnp.concatenate([block_values, jnp.ones((KEYS, HD), BF16)], axis=1))
        places = []
        cache_slot = lane128 % 32
        for i, (_, _, side, part, distance) in enumerate(slot):
            ctx = source_of(side, part, distance)
            places.append(jnp.where(lane128 < SPAN, order[2 * ctx], order[2 * ctx + 1]))
            cache_slot = jnp.where(lane128 // 32 == i, cache_slot + ctx * 32, cache_slot)
        places.append(jnp.where(cache_slot < length[0], -1, 64))
        places = jnp.concatenate(places, axis=1)
        has_diagonal = slot[0][4] == 0
        biases.append(jnp.where(places < my_place, 0.0, HIDDEN))
        if has_diagonal:
            lane = lax.broadcasted_iota(jnp.int32, (1, KEYS), 1) % SPAN
            diagonal = jnp.where(places == my_place, lane, 1000)
        keys.append(block)
    row = lax.broadcasted_iota(jnp.int32, (half_rows, 1), 0) % ROWS + first_row

    def scores_of(h, i):
        s = jnp.dot(q_tiles[h], keys[i], preferred_element_type=F32) * scale
        if slots[i][0][4] == 0:
            return jnp.where(diagonal <= row, s, s + biases[i])
        return s + biases[i]

    tops, accs = [], []
    for h in range(HALVES):
        at = slice(h * half_rows, (h + 1) * half_rows)
        scores = [scores_of(h, i) for i in range(len(slots))]
        pieces = [s[:, i * 128 : (i + 1) * 128] for s in scores for i in range(5)]
        peak = functools.reduce(jnp.maximum, pieces)
        top = jnp.broadcast_to(jnp.max(peak, axis=1, keepdims=True), (half_rows, 128))
        if not first:
            top = jnp.maximum(top_in[at], top)
            factor = jnp.exp2(top_in[at] - top)
            acc = acc_in[at] * jnp.concatenate([factor, factor], axis=1)
        else:
            acc = None
        for i in range(len(slots)):
            weights = jnp.concatenate(
                [jnp.exp2(p - top) for p in pieces[5 * i : 5 * i + 5]], axis=1
            ).astype(BF16)
            added = jnp.dot(weights, values[i], preferred_element_type=F32)
            acc = added if acc is None else acc + added
        tops.append(top)
        accs.append(acc)

    if last:
        for chunk in range(CHUNKS):

            @pl.when(tile // 2 == chunk)
            def _():
                for h in range(HALVES):
                    result = (accs[h][:, :HD] / accs[h][:, HD:]).astype(BF16)
                    for i in range(half_heads):
                        col = (h * half_heads + i) * HD
                        rest[chunk][0, :, col : col + HD] = result[i * ROWS : (i + 1) * ROWS]
    else:
        top_out, acc_out = rest
        for h in range(HALVES):
            top_out[h * half_rows : (h + 1) * half_rows] = tops[h]
            acc_out[h * half_rows : (h + 1) * half_rows] = accs[h]


def attention(meta, order, length, q_own, q_got, kv_blocks, slots, state, last=False):
    first = state is None
    tile_rows = ROWS * GROUP
    tiles = 2 * CHUNKS
    q_spec = pl.BlockSpec((ROWS, WIDTH), lambda step, *_: (step // 2, 0))
    whole = [pl.BlockSpec(b.shape, lambda step, *_: (0, 0, 0)) for b in kv_blocks]
    state_specs = [pl.BlockSpec((tile_rows, w), lambda step, *_: (step, 0)) for w in (HD, 2 * HD)]
    if last:

        def chunk_spec(chunk):
            return pl.BlockSpec((1, ROWS, WIDTH), lambda step, *_: (jnp.clip(step - 2 * chunk, 0, 1), 0, 0))

        out_shape = [jax.ShapeDtypeStruct((2, ROWS, WIDTH), BF16)] * CHUNKS
        out_specs = [chunk_spec(chunk) for chunk in range(CHUNKS)]
    else:
        out_shape = [jax.ShapeDtypeStruct((tiles * tile_rows, w), F32) for w in (HD, 2 * HD)]
        out_specs = state_specs
    work = tiles * tile_rows * KEYS * len(slots)
    return pl.pallas_call(
        functools.partial(attention_kernel, slots=slots, scale=LOG2E / math.sqrt(HD), first=first, last=last),
        out_shape=out_shape,
        grid_spec=pltpu.PrefetchScalarGridSpec(
            num_scalar_prefetch=3,
            grid=(tiles,),
            in_specs=[q_spec, q_spec] + whole + ([] if first else state_specs),
            out_specs=out_specs,
        ),
        compiler_params=pltpu.CompilerParams(vmem_limit_bytes=20 * 1024 * 1024),
        cost_estimate=pl.CostEstimate(flops=work * 32, bytes_accessed=2**18, transcendentals=work // 64),
        name="attention",
    )(meta, order, length, q_own, q_got, *kv_blocks, *([] if first else state))


def parts_of(ref, side, distance, count=4, offset=0):
    return [(ref, i, side, offset + i, distance) for i in range(count)]


def slot_of(meta, s, distance):
    z, y, xhi = meta[1], meta[2], meta[3]
    place = (z + distance + NZ) % NZ
    part = (2 * s + place // 4 - y + 4) % 4
    other = (place // 2 + xhi) % 2
    index = 2 * part + other
    group = jnp.int32(7)
    for position, key in enumerate((4, 3, 5, 6, 0, 1, 2)):
        group = jnp.where(index == key, position, group)
    return 2 * group + place % 2


def place_kernel(meta, *refs, distances):
    n = len(distances)
    sources, out, sem = refs[:n], refs[-2], refs[-1]
    copies = []
    for source, distance in zip(sources, distances):
        for s in range(2):
            row = slot_of(meta, s, distance) * ROWS
            copies.append(
                pltpu.make_async_copy(
                    source.at[s], out.at[pl.ds(pl.multiple_of(row, ROWS), ROWS)], sem.at[len(copies)]
                )
            )
    for c in copies:
        c.start()
    for c in copies:
        c.wait()


def place_rows(meta, sources, distances, rows=None):
    fresh = rows is None
    n = len(sources)
    return pl.pallas_call(
        functools.partial(place_kernel, distances=distances),
        out_shape=jax.ShapeDtypeStruct((16 * ROWS, WIDTH), BF16),
        in_specs=[SMEM_SPEC] + [VMEM_SPEC] * n + ([] if fresh else [pl.BlockSpec(memory_space=pl.ANY)]),
        out_specs=pl.BlockSpec(memory_space=pl.ANY),
        scratch_shapes=[pltpu.SemaphoreType.DMA((2 * n,))],
        input_output_aliases={} if fresh else {n + 1: 0},
        compiler_params=pltpu.CompilerParams(vmem_limit_bytes=4 * 1024 * 1024),
        name="place_rows",
    )(meta, *sources, *([] if fresh else [rows]))


SMEM_SPEC = pl.BlockSpec(memory_space=pltpu.SMEM)
VMEM_SPEC = pl.BlockSpec(memory_space=pltpu.VMEM)


def project_kernel(meta, held, *refs, late, group):
    n = len(late)
    sources, w_refs, outs, rows, sem = refs[:n], refs[n : n + 4], refs[n + 4 : -2], refs[-2], refs[-1]
    mine = pl.ds(group * 8 * ROWS, 8 * ROWS)
    copy = pltpu.make_async_copy(held.at[mine], rows.at[mine], sem)
    copy.start()
    copy.wait()
    for source, (distance, halves) in zip(sources, late):
        for i, s in enumerate(halves):
            row = slot_of(meta, s, distance) * ROWS
            rows[pl.ds(pl.multiple_of(row, ROWS), ROWS)] = source[i]
    for i in range(4):
        total = jnp.dot(rows[mine], w_refs[i][...], preferred_element_type=F32).astype(BF16)
        size = 8 * ROWS // len(outs)
        for k, out in enumerate(outs):
            out[:, 512 * i : 512 * (i + 1)] = total[k * size : (k + 1) * size]


def project(meta, held, late, distances, weights, group):
    count = (2, 4)[group]
    return pl.pallas_call(
        functools.partial(project_kernel, late=distances, group=group),
        out_shape=[jax.ShapeDtypeStruct((8 * ROWS // count, 2048), BF16)] * count,
        in_specs=[SMEM_SPEC, pl.BlockSpec(memory_space=pl.ANY)] + [VMEM_SPEC] * (len(late) + 4),
        out_specs=[VMEM_SPEC] * count,
        scratch_shapes=[pltpu.VMEM((16 * ROWS, WIDTH), BF16), pltpu.SemaphoreType.DMA],
        compiler_params=pltpu.CompilerParams(vmem_limit_bytes=12 * 1024 * 1024),
        cost_estimate=pl.CostEstimate(flops=16 * ROWS * 2048 * 2048, bytes_accessed=1 * 2**20, transcendentals=0),
        name="project",
    )(meta, held, *late, *weights)


def add2(x, y):
    return (x.astype(F32) + y.astype(F32)).astype(BF16)


def last_sum_kernel(x, y, z, u, *outs):
    total = x[...].astype(F32) + y[...].astype(F32) + z[2 * ROWS :].astype(F32) + u[...].astype(F32)
    for i, out in enumerate(outs):
        out[...] = total[:, 512 * i : 512 * (i + 1)].astype(BF16)


def last_sum(*terms):
    return pl.pallas_call(
        last_sum_kernel,
        out_shape=[jax.ShapeDtypeStruct((2 * ROWS, 512), BF16)] * 4,
        in_specs=[VMEM_SPEC] * 4,
        out_specs=[VMEM_SPEC] * 4,
        compiler_params=pltpu.CompilerParams(vmem_limit_bytes=4 * 1024 * 1024),
        name="last_sum",
    )(*terms)


def assemble_kernel(meta, *refs):
    pieces, out = refs[:-1], refs[-1]
    xlo, core = meta[0], meta[1]
    for j in range(CHUNKS):
        for i in range(4):
            from_core = (core + i % 2) % 2
            from_xlo = (xlo + i // 2) % 2
            for zi in range(2):
                row = (zi * 2 + from_core) * 128 + from_xlo * SPAN + j * ROWS
                out[pl.ds(pl.multiple_of(row, 32), ROWS)] = pieces[4 * j + i][zi * ROWS : (zi + 1) * ROWS]


def assemble(meta, pieces):
    return pl.pallas_call(
        assemble_kernel,
        out_shape=jax.ShapeDtypeStruct((512, 512), BF16),
        in_specs=[SMEM_SPEC] + [VMEM_SPEC] * (4 * CHUNKS),
        out_specs=VMEM_SPEC,
        compiler_params=pltpu.CompilerParams(vmem_limit_bytes=4 * 1024 * 1024),
        name="assemble",
    )(meta, *pieces)


def after(value, *others):
    return lax.optimization_barrier((value, *others))[0]


def shards(
    queries, seg_keys, seg_values, cache_keys, cache_values, span_order, cache_length, out_weight
):
    xlo, z, core = lax.axis_index("xlo"), lax.axis_index("z"), lax.axis_index("core")
    y, xhi = lax.axis_index("y"), lax.axis_index("xhi")

    packed = pack(seg_keys, seg_values, cache_keys, cache_values)
    kv_core, kv_xlo, kv_both = flip(packed, "core"), flip(packed, "xlo"), flip_both(packed)
    give = lax.dynamic_slice_in_dim(queries, (1 - xlo) * SPAN, SPAN, 0)
    q_own = lax.dynamic_slice_in_dim(queries, xlo * SPAN, SPAN, 0)
    q_got = flip(after(give, packed), "xlo")
    kv_own = jnp.stack([packed, kv_xlo, kv_core, kv_both])
    paged_keys = seg_keys.reshape(seg_keys.shape[0] // PAGE, PAGE, seg_keys.shape[1])
    page_min, page_max = jnp.min(paged_keys, axis=1), jnp.max(paged_keys, axis=1)
    meta = jnp.stack([xlo, z, core])
    attend = functools.partial(attention, meta, span_order, cache_length, q_own, q_got)
    ring1 = outward(kv_own)
    cross1 = flip(ring1, "core")
    w_gated = after(out_weight, ring1, q_got)
    w_xlo, w_core = flip(w_gated, "xlo"), flip(w_gated, "core")
    ring2 = outward(ring1)
    cross2 = flip(ring2, "core")
    state = attend([kv_own, ring1], [parts_of(0, 0, 0), parts_of(1, 0, 1)], None)
    ring3 = outward(after(ring2, state[0]))
    cross3 = flip(ring3, "core")
    state = attend([ring2, cross1], [parts_of(0, 0, 2), parts_of(1, 1, 1)], state)
    ring4 = outward(after(ring3[:2], state[0], w_core))
    state = attend([ring3, cross2], [parts_of(0, 0, 3), parts_of(1, 1, 2)], state)
    cross4 = flip(after(ring4, state[1]), "core")
    far_slots = [parts_of(0, 1, 3), parts_of(1, 0, 4, 2) + parts_of(2, 1, 4, 2)]
    attended = attend([cross3, ring4, cross4], far_slots, state, True)

    meta_project = after(jnp.stack([xlo, z, y, xhi]), page_min, page_max)

    def both_ways(up, down, *others):
        return shift(after(up, *others), "z", 1), shift(after(down, *others), "z", -1)

    def both_along_y(plus, minus):
        return shift(plus, "y", 1), shift(minus, "y", -1)

    def place_near(own, up, down):
        return place_rows(meta_project, [own, up, down], (0, -1, 1))

    def place_far(rows, up, down):
        return place_rows(meta_project, [up, down], (-2, 2), rows)

    distances = ((-3, (0, 1)), (3, (0, 1)), (4, (0,)), (4, (1,)))
    first, second = attended
    a1 = both_ways(first, first)
    b1 = both_ways(second, second)
    a2 = both_ways(*a1)
    near_a = place_near(first, *a1)
    b2 = both_ways(*b1, near_a)
    a3 = both_ways(*a2, near_a)
    near_b = place_near(second, *b1)
    held_a = place_far(near_a, *a2)
    w_both = flip(after(w_xlo, near_a, near_b, *a2), "core")
    weights = [out_weight, w_core, w_xlo, w_both]
    b3 = both_ways(*b2, near_b)
    a4 = both_ways(a3[0][:1], a3[1][1:], held_a)
    held_b = place_far(near_b, *b2)
    b4 = both_ways(b3[0][:1], b3[1][1:], held_b)
    late_a, late_b = [*a3, *a4], [*b3, *b4]
    project_rows = functools.partial(project, meta_project)

    plus_a, minus_a = project_rows(after(held_a, *b3, held_b), late_a, distances, weights, 0)
    plus_b, minus_b = project_rows(after(held_b, plus_a), late_b, distances, weights, 0)
    sums_a, sums_b = both_along_y(plus_a, minus_a), both_along_y(plus_b, minus_b)
    rest_a = project_rows(held_a, late_a, distances, weights, 1)
    rest_b = project_rows(after(held_b, *sums_a), late_b, distances, weights, 1)

    pieces = []
    for (plus, minus), (own_a, own_b, p1a, p3b) in ((sums_a, rest_a), (sums_b, rest_b)):
        in1a, in3b = both_along_y(add2(p1a, plus[: 2 * ROWS]), add2(p3b, minus[: 2 * ROWS]))
        give_b = (own_b.astype(F32) + plus[2 * ROWS :].astype(F32) + in3b.astype(F32)).astype(BF16)
        got_a = flip(give_b, "xhi")
        mine, to_core, to_xlo, to_both = last_sum(own_a, in1a, minus, got_a)
        pieces += [mine, flip(to_core, "core"), flip(to_xlo, "xlo"), flip_both(to_both)]
    mixed = assemble(jnp.stack([xlo, core]), pieces)
    return (mixed, page_min, page_max)


def solution(mesh):
    split = Mesh(mesh.devices.reshape(2, NZ, 2, 4, 2), ("xlo", "z", "core", "y", "xhi"))
    ctx, head = ("xlo", "z", "core"), ("y", "xhi")
    in_specs = (
        P(ctx, head),
        P(ctx, head),
        P(ctx, head),
        P(ctx, head),
        P(ctx, head),
        P(),
        P(),
        P(head, ctx),
    )
    out_specs = (P(head, ctx), P(ctx, head), P(ctx, head))
    return jax.shard_map(shards, mesh=split, in_specs=in_specs, out_specs=out_specs, check_vma=False)
```

```python
import functools
import math

import jax
import jax.numpy as jnp
from jax import lax
from jax.experimental import pallas as pl
from jax.experimental.pallas import tpu as pltpu
from jax.sharding import Mesh
from jax.sharding import PartitionSpec as P

HD = 128
GROUP = 16
PAGE = 16
SPAN = 64
NZ = 8
CHUNKS = 2
ROWS = SPAN // CHUNKS
WIDTH = GROUP * HD
LOG2E = 1.4426950408889634
HIDDEN = -1e30
KEYS = 640
HALVES = 2
F32 = jnp.float32
BF16 = jnp.bfloat16


def shift(block, axis, distance):
    n = lax.axis_size(axis)
    return lax.ppermute(block, axis, [(i, (i + distance) % n) for i in range(n)])


def flip(block, axis):
    return shift(block, axis, 1)


def flip_both(block):
    return lax.ppermute(block, ("xlo", "core"), [(i, 3 - i) for i in range(4)])


def outward(block):
    route = []
    for z in range(NZ):
        route.append((2 * z, 2 * ((z + 1) % NZ)))
        route.append((2 * z + 1, 2 * ((z - 1) % NZ) + 1))
    return lax.ppermute(block, ("z", "core"), route)


def pack_kernel(k, v, ck, cv, out):
    out[0:128] = k[...].T
    out[128:256] = v[...]
    out[256:288] = ck[...]
    out[288:320] = cv[...]


def pack(k, v, ck, cv):
    return pl.pallas_call(
        pack_kernel,
        out_shape=jax.ShapeDtypeStruct((320, HD), BF16),
        name="pack",
    )(k, v, ck, cv)


def attention_kernel(meta, order, length, q_own, q_got, *rest, slots, scale, first, last):
    n_refs = 1 + max(part[0] for slot in slots for part in slot)
    kv_refs, rest = rest[:n_refs], rest[n_refs:]
    if not first:
        top_in, acc_in, rest = rest[0], rest[1], rest[2:]
    tile = pl.program_id(0)
    span = tile % 2
    xlo, z, core = meta[0], meta[1], meta[2]
    first_row = tile // 2 * ROWS
    lane128 = lax.broadcasted_iota(jnp.int32, (1, 128), 1)

    def source_of(side, part, distance):
        sign = jnp.where((core + side) % 2 == 0, -1, 1)
        sz = (z + sign * distance + NZ) % NZ
        return ((xlo + part % 2) % 2) * 16 + sz * 2 + (core + part // 2 + side) % 2

    own_place = order[2 * (xlo * 16 + z * 2 + core) + xlo]
    got_place = order[2 * ((1 - xlo) * 16 + z * 2 + core) + xlo]
    mine = span == xlo
    my_place = jnp.where(mine, own_place, got_place)
    q_rows = jnp.where(mine, q_own[...], q_got[...])
    half_heads = GROUP // HALVES
    half_rows = half_heads * ROWS
    q_tiles = [
        jnp.concatenate([q_rows[:, i * HD : (i + 1) * HD] for i in range(h * half_heads, (h + 1) * half_heads)], axis=0)
        for h in range(HALVES)
    ]

    keys, values, biases, diagonal = [], [], [], None
    for slot in slots:
        parts = [kv_refs[ref].at[place] for ref, place, *_ in slot]
        block = jnp.concatenate(
            [p[0:128] for p in parts] + [jnp.concatenate([p[256:288] for p in parts], axis=0).T], axis=1
        )
        block_values = jnp.concatenate([p[128:256] for p in parts] + [p[288:320] for p in parts], axis=0)
        values.append(jnp.concatenate([block_values, jnp.ones((KEYS, HD), BF16)], axis=1))
        places = []
        cache_slot = lane128 % 32
        for i, (_, _, side, part, distance) in enumerate(slot):
            ctx = source_of(side, part, distance)
            places.append(jnp.where(lane128 < SPAN, order[2 * ctx], order[2 * ctx + 1]))
            cache_slot = jnp.where(lane128 // 32 == i, cache_slot + ctx * 32, cache_slot)
        places.append(jnp.where(cache_slot < length[0], -1, 64))
        places = jnp.concatenate(places, axis=1)
        has_diagonal = slot[0][4] == 0
        biases.append(jnp.where(places < my_place, 0.0, HIDDEN))
        if has_diagonal:
            lane = lax.broadcasted_iota(jnp.int32, (1, KEYS), 1) % SPAN
            diagonal = jnp.where(places == my_place, lane, 1000)
        keys.append(block)
    row = lax.broadcasted_iota(jnp.int32, (half_rows, 1), 0) % ROWS + first_row

    def scores_of(h, i):
        s = jnp.dot(q_tiles[h], keys[i], preferred_element_type=F32) * scale
        if slots[i][0][4] == 0:
            return jnp.where(diagonal <= row, s, s + biases[i])
        return s + biases[i]

    tops, accs = [], []
    for h in range(HALVES):
        at = slice(h * half_rows, (h + 1) * half_rows)
        scores = [scores_of(h, i) for i in range(len(slots))]
        pieces = [s[:, i * 128 : (i + 1) * 128] for s in scores for i in range(5)]
        peak = functools.reduce(jnp.maximum, pieces)
        top = jnp.broadcast_to(jnp.max(peak, axis=1, keepdims=True), (half_rows, 128))
        if not first:
            top = jnp.maximum(top_in[at], top)
            factor = jnp.exp2(top_in[at] - top)
            acc = acc_in[at] * jnp.concatenate([factor, factor], axis=1)
        else:
            acc = None
        for i in range(len(slots)):
            weights = jnp.concatenate(
                [jnp.exp2(p - top) for p in pieces[5 * i : 5 * i + 5]], axis=1
            ).astype(BF16)
            added = jnp.dot(weights, values[i], preferred_element_type=F32)
            acc = added if acc is None else acc + added
        tops.append(top)
        accs.append(acc)

    if last:
        for chunk in range(CHUNKS):

            @pl.when(tile // 2 == chunk)
            def _():
                for h in range(HALVES):
                    result = (accs[h][:, :HD] / accs[h][:, HD:]).astype(BF16)
                    for i in range(half_heads):
                        col = (h * half_heads + i) * HD
                        rest[chunk][0, :, col : col + HD] = result[i * ROWS : (i + 1) * ROWS]
    else:
        top_out, acc_out = rest
        for h in range(HALVES):
            top_out[h * half_rows : (h + 1) * half_rows] = tops[h]
            acc_out[h * half_rows : (h + 1) * half_rows] = accs[h]


def attention(meta, order, length, q_own, q_got, kv_blocks, slots, state, last=False):
    first = state is None
    tile_rows = ROWS * GROUP
    tiles = 2 * CHUNKS
    q_spec = pl.BlockSpec((ROWS, WIDTH), lambda step, *_: (step // 2, 0))
    whole = [pl.BlockSpec(b.shape, lambda step, *_: (0, 0, 0)) for b in kv_blocks]
    state_specs = [pl.BlockSpec((tile_rows, w), lambda step, *_: (step, 0)) for w in (HD, 2 * HD)]
    if last:

        def chunk_spec(chunk):
            return pl.BlockSpec((1, ROWS, WIDTH), lambda step, *_: (jnp.clip(step - 2 * chunk, 0, 1), 0, 0))

        out_shape = [jax.ShapeDtypeStruct((2, ROWS, WIDTH), BF16)] * CHUNKS
        out_specs = [chunk_spec(chunk) for chunk in range(CHUNKS)]
    else:
        out_shape = [jax.ShapeDtypeStruct((tiles * tile_rows, w), F32) for w in (HD, 2 * HD)]
        out_specs = state_specs
    work = tiles * tile_rows * KEYS * len(slots)
    return pl.pallas_call(
        functools.partial(attention_kernel, slots=slots, scale=LOG2E / math.sqrt(HD), first=first, last=last),
        out_shape=out_shape,
        grid_spec=pltpu.PrefetchScalarGridSpec(
            num_scalar_prefetch=3,
            grid=(tiles,),
            in_specs=[q_spec, q_spec] + whole + ([] if first else state_specs),
            out_specs=out_specs,
        ),
        compiler_params=pltpu.CompilerParams(vmem_limit_bytes=20 * 1024 * 1024),
        cost_estimate=pl.CostEstimate(flops=work * 32, bytes_accessed=2**18, transcendentals=work // 64),
        name="attention",
    )(meta, order, length, q_own, q_got, *kv_blocks, *([] if first else state))


def parts_of(ref, side, distance, count=4, offset=0):
    return [(ref, i, side, offset + i, distance) for i in range(count)]


def slot_of(meta, s, distance):
    z, y, xhi = meta[1], meta[2], meta[3]
    place = (z + distance + NZ) % NZ
    part = (2 * s + place // 4 - y + 4) % 4
    other = (place // 2 + xhi) % 2
    index = 2 * part + other
    group = jnp.int32(7)
    for position, key in enumerate((4, 3, 5, 6, 0, 1, 2)):
        group = jnp.where(index == key, position, group)
    return 2 * group + place % 2


def place_kernel(meta, *refs, distances):
    n = len(distances)
    sources, out, sem = refs[:n], refs[-2], refs[-1]
    copies = []
    for source, distance in zip(sources, distances):
        for s in range(2):
            row = slot_of(meta, s, distance) * ROWS
            copies.append(
                pltpu.make_async_copy(
                    source.at[s], out.at[pl.ds(pl.multiple_of(row, ROWS), ROWS)], sem.at[len(copies)]
                )
            )
    for c in copies:
        c.start()
    for c in copies:
        c.wait()


def place_rows(meta, sources, distances, rows=None):
    fresh = rows is None
    n = len(sources)
    return pl.pallas_call(
        functools.partial(place_kernel, distances=distances),
        out_shape=jax.ShapeDtypeStruct((16 * ROWS, WIDTH), BF16),
        in_specs=[SMEM_SPEC] + [VMEM_SPEC] * n + ([] if fresh else [pl.BlockSpec(memory_space=pl.ANY)]),
        out_specs=pl.BlockSpec(memory_space=pl.ANY),
        scratch_shapes=[pltpu.SemaphoreType.DMA((2 * n,))],
        input_output_aliases={} if fresh else {n + 1: 0},
        compiler_params=pltpu.CompilerParams(vmem_limit_bytes=4 * 1024 * 1024),
        name="place_rows",
    )(meta, *sources, *([] if fresh else [rows]))


SMEM_SPEC = pl.BlockSpec(memory_space=pltpu.SMEM)
VMEM_SPEC = pl.BlockSpec(memory_space=pltpu.VMEM)


def project_kernel(meta, held, *refs, late, group):
    n = len(late)
    sources, w_refs, outs, rows, sem = refs[:n], refs[n : n + 4], refs[n + 4 : -2], refs[-2], refs[-1]
    mine = pl.ds(group * 8 * ROWS, 8 * ROWS)
    copy = pltpu.make_async_copy(held.at[mine], rows.at[mine], sem)
    copy.start()
    copy.wait()
    for source, (distance, halves) in zip(sources, late):
        for i, s in enumerate(halves):
            row = slot_of(meta, s, distance) * ROWS
            rows[pl.ds(pl.multiple_of(row, ROWS), ROWS)] = source[i]
    for i in range(4):
        total = jnp.dot(rows[mine], w_refs[i][...], preferred_element_type=F32).astype(BF16)
        size = 8 * ROWS // len(outs)
        for k, out in enumerate(outs):
            out[:, 512 * i : 512 * (i + 1)] = total[k * size : (k + 1) * size]


def project(meta, held, late, distances, weights, group):
    count = (2, 4)[group]
    return pl.pallas_call(
        functools.partial(project_kernel, late=distances, group=group),
        out_shape=[jax.ShapeDtypeStruct((8 * ROWS // count, 2048), BF16)] * count,
        in_specs=[SMEM_SPEC, pl.BlockSpec(memory_space=pl.ANY)] + [VMEM_SPEC] * (len(late) + 4),
        out_specs=[VMEM_SPEC] * count,
        scratch_shapes=[pltpu.VMEM((16 * ROWS, WIDTH), BF16), pltpu.SemaphoreType.DMA],
        compiler_params=pltpu.CompilerParams(vmem_limit_bytes=12 * 1024 * 1024),
        cost_estimate=pl.CostEstimate(flops=16 * ROWS * 2048 * 2048, bytes_accessed=1 * 2**20, transcendentals=0),
        name="project",
    )(meta, held, *late, *weights)


def add2(x, y):
    return (x.astype(F32) + y.astype(F32)).astype(BF16)


def last_sum_kernel(x, y, z, u, *outs):
    total = x[...].astype(F32) + y[...].astype(F32) + z[2 * ROWS :].astype(F32) + u[...].astype(F32)
    for i, out in enumerate(outs):
        out[...] = total[:, 512 * i : 512 * (i + 1)].astype(BF16)


def last_sum(*terms):
    return pl.pallas_call(
        last_sum_kernel,
        out_shape=[jax.ShapeDtypeStruct((2 * ROWS, 512), BF16)] * 4,
        in_specs=[VMEM_SPEC] * 4,
        out_specs=[VMEM_SPEC] * 4,
        compiler_params=pltpu.CompilerParams(vmem_limit_bytes=4 * 1024 * 1024),
        name="last_sum",
    )(*terms)


def assemble_kernel(meta, *refs):
    pieces, out = refs[:-1], refs[-1]
    xlo, core = meta[0], meta[1]
    for j in range(CHUNKS):
        for i in range(4):
            from_core = (core + i % 2) % 2
            from_xlo = (xlo + i // 2) % 2
            for zi in range(2):
                row = (zi * 2 + from_core) * 128 + from_xlo * SPAN + j * ROWS
                out[pl.ds(pl.multiple_of(row, 32), ROWS)] = pieces[4 * j + i][zi * ROWS : (zi + 1) * ROWS]


def assemble(meta, pieces):
    return pl.pallas_call(
        assemble_kernel,
        out_shape=jax.ShapeDtypeStruct((512, 512), BF16),
        in_specs=[SMEM_SPEC] + [VMEM_SPEC] * (4 * CHUNKS),
        out_specs=VMEM_SPEC,
        compiler_params=pltpu.CompilerParams(vmem_limit_bytes=4 * 1024 * 1024),
        name="assemble",
    )(meta, *pieces)


def after(value, *others):
    return lax.optimization_barrier((value, *others))[0]


def shards(
    queries, seg_keys, seg_values, cache_keys, cache_values, span_order, cache_length, out_weight
):
    xlo, z, core = lax.axis_index("xlo"), lax.axis_index("z"), lax.axis_index("core")
    y, xhi = lax.axis_index("y"), lax.axis_index("xhi")

    packed = pack(seg_keys, seg_values, cache_keys, cache_values)
    kv_core, kv_xlo, kv_both = flip(packed, "core"), flip(packed, "xlo"), flip_both(packed)
    give = lax.dynamic_slice_in_dim(queries, (1 - xlo) * SPAN, SPAN, 0)
    q_own = lax.dynamic_slice_in_dim(queries, xlo * SPAN, SPAN, 0)
    q_got = flip(after(give, packed), "xlo")
    kv_own = jnp.stack([packed, kv_xlo, kv_core, kv_both])
    paged_keys = seg_keys.reshape(seg_keys.shape[0] // PAGE, PAGE, seg_keys.shape[1])
    page_min, page_max = jnp.min(paged_keys, axis=1), jnp.max(paged_keys, axis=1)
    meta = jnp.stack([xlo, z, core])
    attend = functools.partial(attention, meta, span_order, cache_length, q_own, q_got)
    ring1 = outward(kv_own)
    cross1 = flip(ring1, "core")
    w_gated = after(out_weight, ring1, q_got)
    w_xlo, w_core = flip(w_gated, "xlo"), flip(w_gated, "core")
    ring2 = outward(ring1)
    cross2 = flip(ring2, "core")
    state = attend([kv_own, ring1], [parts_of(0, 0, 0), parts_of(1, 0, 1)], None)
    ring3 = outward(after(ring2, state[0]))
    cross3 = flip(ring3, "core")
    state = attend([ring2, cross1], [parts_of(0, 0, 2), parts_of(1, 1, 1)], state)
    ring4 = outward(after(ring3[:2], state[0], w_core))
    state = attend([ring3, cross2], [parts_of(0, 0, 3), parts_of(1, 1, 2)], state)
    cross4 = flip(after(ring4, state[1]), "core")
    far_slots = [parts_of(0, 1, 3), parts_of(1, 0, 4, 2) + parts_of(2, 1, 4, 2)]
    attended = attend([cross3, ring4, cross4], far_slots, state, True)

    meta_project = after(jnp.stack([xlo, z, y, xhi]), page_min, page_max)

    def both_ways(up, down, *others):
        return shift(after(up, *others), "z", 1), shift(after(down, *others), "z", -1)

    def both_along_y(plus, minus):
        return shift(plus, "y", 1), shift(minus, "y", -1)

    def place_near(own, up, down):
        return place_rows(meta_project, [own, up, down], (0, -1, 1))

    def place_far(rows, up, down):
        return place_rows(meta_project, [up, down], (-2, 2), rows)

    distances = ((-3, (0, 1)), (3, (0, 1)), (4, (0,)), (4, (1,)))
    first, second = attended
    a1 = both_ways(first, first)
    b1 = both_ways(second, second)
    a2 = both_ways(*a1)
    near_a = place_near(first, *a1)
    b2 = both_ways(*b1, near_a)
    a3 = both_ways(*a2, near_a)
    near_b = place_near(second, *b1)
    held_a = place_far(near_a, *a2)
    w_both = flip(after(w_xlo, near_a, near_b, *a2), "core")
    weights = [out_weight, w_core, w_xlo, w_both]
    b3 = both_ways(*b2, near_b)
    a4 = both_ways(a3[0][:1], a3[1][1:], held_a)
    held_b = place_far(near_b, *b2)
    b4 = both_ways(b3[0][:1], b3[1][1:], held_b)
    late_a, late_b = [*a3, *a4], [*b3, *b4]
    project_rows = functools.partial(project, meta_project)

    plus_a, minus_a = project_rows(after(held_a, *b3, held_b), late_a, distances, weights, 0)
    plus_b, minus_b = project_rows(after(held_b, plus_a), late_b, distances, weights, 0)
    sums_a, sums_b = both_along_y(plus_a, minus_a), both_along_y(plus_b, minus_b)
    rest_a = project_rows(held_a, late_a, distances, weights, 1)
    rest_b = project_rows(after(held_b, *sums_a), late_b, distances, weights, 1)

    pieces = []
    for (plus, minus), (own_a, own_b, p1a, p3b) in ((sums_a, rest_a), (sums_b, rest_b)):
        in1a, in3b = both_along_y(add2(p1a, plus[: 2 * ROWS]), add2(p3b, minus[: 2 * ROWS]))
        give_b = (after(own_b, in1a).astype(F32) + plus[2 * ROWS :].astype(F32) + in3b.astype(F32)).astype(BF16)
        got_a = flip(give_b, "xhi")
        mine, to_core, to_xlo, to_both = last_sum(own_a, in1a, minus, got_a)
        pieces += [mine, flip(to_core, "core"), flip(to_xlo, "xlo"), flip_both(to_both)]
    mixed = assemble(jnp.stack([xlo, core]), pieces)
    return (mixed, page_min, page_max)


def solution(mesh):
    split = Mesh(mesh.devices.reshape(2, NZ, 2, 4, 2), ("xlo", "z", "core", "y", "xhi"))
    ctx, head = ("xlo", "z", "core"), ("y", "xhi")
    in_specs = (
        P(ctx, head),
        P(ctx, head),
        P(ctx, head),
        P(ctx, head),
        P(ctx, head),
        P(),
        P(),
        P(head, ctx),
    )
    out_specs = (P(head, ctx), P(ctx, head), P(ctx, head))
    return jax.shard_map(shards, mesh=split, in_specs=in_specs, out_specs=out_specs, check_vma=False)
```
